256 devices in a mesh: ctx: 16 (over z_lo, x, core), exp: 16 (over z_hi, y).
Axes of the slice: x: 4, y: 4, z: 8 (z_hi: 4, z_lo: 2; z = z_hi * 2 + z_lo), core: 2. Of those that a mesh axis runs over, the one named last changes fastest.
Arguments:
- queries: bfloat16 [16, 2048, 1536], P('exp', 'ctx'), may hold values from -2.5 to 2.5
- key_states: bfloat16 [16, 2048, 1536], P('exp', 'ctx'), may hold values from -2.5 to 2.5
- value_states: bfloat16 [16, 2048, 1536], P('exp', 'ctx'), may hold values from -6 to 6
- attended: bfloat16 [16, 2048, 1536], P('exp', 'ctx'), may hold values from -6 to 6
- output_grad: bfloat16 [16, 2048, 1536], P('exp', 'ctx'), may hold values from -6 to 6
- expert_ids: int32 [16, 2048, 2], P('exp', 'ctx'), may hold values from 0 to 15, all different within a row; in each aligned block of 128 rows (0 to 127, 128 to 255, ..., all dimensions but the last counted through in order) at most 24 rows name the same one
- gate_weights: float32 [16, 2048, 2], P('exp', 'ctx'), may hold values from 0.2 to 1
- w_in: bfloat16 [16, 1536, 768], P('exp'), may hold values from -0.15625 to 0.15625
- w_out: bfloat16 [16, 768, 1536], P('exp'), may hold values from -0.21875 to 0.21875
Outputs:
- query_grad: bfloat16 [16, 2048, 1536], P('exp', 'ctx')
- key_grad: bfloat16 [16, 2048, 1536], P('exp', 'ctx')
- value_grad: bfloat16 [16, 2048, 1536], P('exp', 'ctx')
- w_in_grad: bfloat16 [16, 1536, 768], P('exp', 'ctx')
- w_out_grad: bfloat16 [16, 768, 1536], P('exp', 'ctx')
The draws below stay inside these ranges and needn't reach their ends.
Inputs may be any that keep to these rules, and one draw needn't show every extreme that they name: `expert_ids`: in each aligned block of 128 frames (the frames of one device) no expert is named by more than 24 frames, a bound that some block reaches; the two experts of a frame differ.
All inputs are finite; a program needn't handle non-finite values.
Results may differ from the reference program's by a relative error of at most 0.02.
Values may be sent and summed in bfloat16 or wider, within the bound.
A program may use at most 128 MiB of HBM per device.

```python
import math
import jax
import jax.numpy as jnp
import numpy as np
from jax import lax

HEADS = 12
HEAD_DIM = 128
D = 1536
FF = 768
TOK = 128
EXPERTS = 16
BATCH = 16
LEN = 2048
CAP = 24
N_CTX = 16


def shard_levels(rng, dims, pieces, smallest, high):
    level, own = 1.0, jax.random.fold_in(rng, 6)
    for position, blocks in pieces:
        steps = jnp.exp(jax.random.uniform(jax.random.fold_in(own, position), (blocks,), jnp.float32, smallest / len(pieces), high / len(pieces)))
        level = level * jnp.repeat(steps, dims[position] // blocks).reshape([-1 if axis == position else 1 for axis in range(len(dims))])
    return level


def shared_out(rng, own, number, rows, number_of, top, reach, skew):
    order = jax.random.permutation(rng, number_of)
    heavy_load, ordinary = shares(number_of, rows * top, reach, skew, True), shares(number_of, rows * top, reach, skew, False)
    places = jnp.arange(number_of)

    def named(tallies, turn):
        used = int((tallies > 0).sum())
        fixed = max(1, used // 4)
        shifted = fixed + (places - fixed + turn * (used - fixed)) % max(1, number_of - fixed)
        return jnp.zeros((number_of,), jnp.int32).at[order[jnp.where(places < fixed, places, shifted)]].set(jnp.asarray(tallies, jnp.int32))

    tallies = jnp.where(number % 4 == 0, named(heavy_load, number // 4), named(ordinary, number - number // 4 - 1))
    mixed = jax.random.permutation(jax.random.fold_in(own, 3), number_of)
    donor, receiver = mixed[0:number_of // 2 * 2:2], mixed[1:number_of // 2 * 2:2]
    slack = jnp.minimum(tallies[donor] - 1, reach - tallies[receiver]) // 2
    slack = jnp.where((donor == order[0]) | (receiver == order[0]) | (tallies[receiver] == 0), 0, jnp.maximum(slack, 0))
    shifted = jax.random.randint(jax.random.fold_in(own, 4), (number_of // 2,), 0, 1 << 20) % (slack + 1)
    tallies = tallies.at[donor].add(-shifted).at[receiver].add(shifted)
    items = jnp.searchsorted(jnp.cumsum(tallies), jnp.arange(rows * top), side="right").astype(jnp.int32)
    table = items.reshape(top, rows).T
    table = table[jax.random.permutation(jax.random.fold_in(own, 1), rows)]
    turn = jax.random.randint(jax.random.fold_in(own, 2), (rows, 1), 0, top)
    return jnp.take_along_axis(table, (jnp.arange(top)[None, :] + turn) % top, axis=1)


def shares(count, total, reach, lean, full):
    weights = [(1 << 20) // math.isqrt(standing ** lean) + 1 for standing in range(1, count + 1)]
    largest = reach if full else min(reach, max(-(-total // count), total * weights[0] // sum(weights)))
    least = 1 if total - largest >= count - 1 else 0
    given, spare = [largest] + [least] * (count - 1), total - largest - least * (count - 1)
    while spare > 0:
        free = [i for i in range(1, count) if given[i] < largest] or [i for i in range(1, count) if given[i] < reach]
        mass, budget = sum([weights[i] for i in free]), spare
        for i in free:
            addition = min(reach - given[i], max(1, budget * weights[i] // mass), spare)
            given[i] = given[i] + addition
            spare = spare - addition
    return np.array(given)


def bell_draw(key, extent, scale, most, cuts=(), held_as=jnp.bfloat16):
    array = jax.random.normal(key, extent, jnp.float32) * scale
    if len(cuts) > 0:
        array = shard_levels(key, extent, cuts, -0.22, 0.18) * array
    return jnp.clip(array, min=-most, max=most).astype(held_as)


def setup_inputs(seed: int = 0) -> dict:
    key_list = jax.random.split(jax.random.key(seed), 10)
    queries = bell_draw(key_list[0], (BATCH, LEN, D), 1.0, 2.5, ((0, 16), (1, 16)))
    key_states = bell_draw(key_list[1], (BATCH, LEN, D), 1.0, 2.5, ((0, 16), (1, 16)))
    value_states = bell_draw(key_list[2], (BATCH, LEN, D), 1.0, 6.0, ((0, 16), (1, 16)))
    attended = bell_draw(key_list[3], (BATCH, LEN, D), 1.0, 6.0, ((0, 16), (1, 16)))
    output_grad = bell_draw(key_list[4], (BATCH, LEN, D), 1.0, 6.0, ((0, 16), (1, 16)))
    expert_ids_keys = jax.random.split(jax.random.fold_in(key_list[5], 1), BATCH * LEN // TOK)
    expert_ids_turns = jax.random.permutation(jax.random.fold_in(key_list[5], 3), BATCH * LEN // TOK)
    expert_ids = jax.vmap(lambda own, number: shared_out(jax.random.fold_in(key_list[5], 2), own, number, TOK, EXPERTS, 2, CAP, 2))(expert_ids_keys, expert_ids_turns).reshape((BATCH, LEN, 2))
    gate_weights = jnp.clip(0.2 + 0.8 * jax.random.uniform(key_list[6], (BATCH, LEN, 2), jnp.float32) ** shard_levels(key_list[6], (BATCH, LEN, 2), ((0, 16), (1, 16)), -0.2, 0.2), 0.2, 1.0)
    w_in = bell_draw(key_list[7], (EXPERTS, D, FF), D ** -0.5, 0.15625, ((0, 16),))
    w_out = bell_draw(key_list[8], (EXPERTS, FF, D), FF ** -0.5, 0.21875, ((0, 16),))
    return {"queries": queries, "key_states": key_states, "value_states": value_states, "attended": attended, "output_grad": output_grad, "expert_ids": expert_ids, "gate_weights": gate_weights, "w_in": w_in, "w_out": w_out}


def rounded(x):
    return lax.optimization_barrier(x.astype(jnp.bfloat16)).astype(jnp.float32)


def expert_part(attended, output_grad, expert_ids, gate_weights, w_in, w_out):
    flat_rows = attended.reshape(-1, D)
    flat_grad = output_grad.reshape(-1, D)
    nrows = flat_rows.shape[0]
    nblocks = nrows // TOK
    route = expert_ids.reshape(nblocks, TOK * 2).astype(jnp.int32)
    onehot = (route[:, :, None] == jnp.arange(EXPERTS, dtype=jnp.int32)[None, None, :]).astype(jnp.int32)
    slot = jnp.sum((jnp.cumsum(onehot, axis=1) - 1) * onehot, axis=2).astype(jnp.int32)
    pair_expert = route.reshape(-1)
    pair_slot = slot.reshape(-1)
    pair_index = jnp.arange(nblocks * TOK * 2, dtype=jnp.int32)
    pair_block = pair_index // (TOK * 2)
    pair_row = pair_index // 2
    rows_buf = jnp.zeros((EXPERTS, nblocks, CAP, D), jnp.bfloat16)
    rows_buf = rows_buf.at[pair_expert, pair_block, pair_slot].set(flat_rows[pair_row])
    row_grad = (gate_weights.reshape(-1)[:, None] * flat_grad[pair_row].astype(jnp.float32)).astype(jnp.bfloat16)
    grad_buf = jnp.zeros((EXPERTS, nblocks, CAP, D), jnp.bfloat16)
    grad_buf = grad_buf.at[pair_expert, pair_block, pair_slot].set(row_grad)

    def one_expert(item):
        rows, grads, w_first, w_second = item
        upper = jnp.einsum("ncd,df->ncf", rows.astype(jnp.float32), w_first.astype(jnp.float32))
        sig = jax.nn.sigmoid(upper)
        act = (upper * sig).astype(jnp.bfloat16)
        act_grad = jnp.einsum("ncd,fd->ncf", grads.astype(jnp.float32), w_second.astype(jnp.float32))
        up_grad = (act_grad * sig * (1.0 + upper * (1.0 - sig))).astype(jnp.bfloat16)
        row_back = jnp.einsum("ncf,df->ncd", up_grad.astype(jnp.float32), w_first.astype(jnp.float32)).astype(jnp.bfloat16)
        rows_c = rows.reshape(BATCH, N_CTX, CAP, D).astype(jnp.float32)
        grads_c = grads.reshape(BATCH, N_CTX, CAP, D).astype(jnp.float32)
        upg_c = up_grad.reshape(BATCH, N_CTX, CAP, FF).astype(jnp.float32)
        act_c = act.reshape(BATCH, N_CTX, CAP, FF).astype(jnp.float32)
        first_grad = jnp.sum(rounded(jnp.einsum("bcsd,bcsf->cdf", rows_c, upg_c)), axis=0).astype(jnp.bfloat16)
        second_grad = jnp.sum(rounded(jnp.einsum("bcsf,bcsd->cfd", act_c, grads_c)), axis=0).astype(jnp.bfloat16)
        return row_back, first_grad, second_grad

    back_buf, w_in_grad, w_out_grad = lax.map(one_expert, (rows_buf, grad_buf, w_in, w_out))
    back = back_buf[pair_expert, pair_block, pair_slot].astype(jnp.float32).reshape(nrows, 2, D)
    attn_grad = (flat_grad.astype(jnp.float32) + back[:, 0] + back[:, 1]).astype(jnp.bfloat16)
    return attn_grad.reshape(BATCH, LEN, D), w_in_grad, w_out_grad


def attention_stream(item):
    queries, key_states, value_states, attended, attn_grad = item
    scale = HEAD_DIM ** -0.5
    q_all = queries.astype(jnp.float32).reshape(N_CTX, TOK, HEADS, HEAD_DIM)
    k_all = key_states.astype(jnp.float32).reshape(LEN, HEADS, HEAD_DIM)
    v_all = value_states.astype(jnp.float32).reshape(LEN, HEADS, HEAD_DIM)
    k_blocks = k_all.reshape(N_CTX, TOK, HEADS, HEAD_DIM)
    g_all = attn_grad.astype(jnp.float32).reshape(N_CTX, TOK, HEADS, HEAD_DIM)
    delta_all = jnp.sum(g_all * attended.astype(jnp.float32).reshape(N_CTX, TOK, HEADS, HEAD_DIM), axis=3)

    def step(carry, blk):
        key_acc, value_acc = carry
        q_blk, g_blk, d_blk = blk
        scores = jnp.einsum("qhd,khd->hqk", q_blk, k_all) * scale
        norm_log = jnp.log(jnp.sum(jnp.exp(scores), axis=2))
        probs = jnp.exp(scores - norm_log[:, :, None])
        probs_b = probs.astype(jnp.bfloat16).astype(jnp.float32)
        prob_grad = jnp.einsum("qhd,khd->hqk", g_blk, v_all)
        score_grad = (probs * (prob_grad - d_blk.T[:, :, None])).astype(jnp.bfloat16).astype(jnp.float32)
        split = score_grad.reshape(HEADS, TOK, N_CTX, TOK)
        q_part = jnp.einsum("hqck,ckhd->cqhd", split, k_blocks) * scale
        q_grad = jnp.sum(rounded(q_part), axis=0).astype(jnp.bfloat16)
        key_acc = key_acc + rounded(jnp.einsum("hqk,qhd->khd", score_grad, q_blk) * scale)
        value_acc = value_acc + rounded(jnp.einsum("hqk,qhd->khd", probs_b, g_blk))
        return (key_acc, value_acc), q_grad

    zero = jnp.zeros((LEN, HEADS, HEAD_DIM), jnp.float32)
    (key_acc, value_acc), q_grads = lax.scan(step, (zero, zero), (q_all, g_all, delta_all))
    return (q_grads.reshape(LEN, D), key_acc.reshape(LEN, D).astype(jnp.bfloat16),
            value_acc.reshape(LEN, D).astype(jnp.bfloat16))


def reference(queries, key_states, value_states, attended, output_grad, expert_ids, gate_weights, w_in, w_out):
    attn_grad, w_in_grad, w_out_grad = expert_part(attended, output_grad, expert_ids, gate_weights, w_in, w_out)
    query_grad, key_grad, value_grad = lax.map(attention_stream, (queries, key_states, value_states, attended, attn_grad))
    return query_grad, key_grad, value_grad, w_in_grad, w_out_grad
```

```python
import functools

import jax
import jax.numpy as jnp
from jax import lax
from jax.experimental import pallas as pl
from jax.experimental.pallas import tpu as pltpu
from jax.sharding import PartitionSpec as P

HEAD_DIM = 128
MESH = pl.DeviceIdType.MESH
F32 = jnp.float32
BF16 = jnp.bfloat16


def dot_nn(a, b):
    return lax.dot_general(a, b, (((1,), (0,)), ((), ())), preferred_element_type=F32)


def dot_nt(a, b):
    return lax.dot_general(a, b, (((1,), (1,)), ((), ())), preferred_element_type=F32)


def dot_tn(a, b):
    return lax.dot_general(a, b, (((0,), (0,)), ((), ())), preferred_element_type=F32)


def kernel(
    nx, nexp, group,
    ids_ref, gates_ref, q_ref, k_ref, v_ref, att_ref, og_ref, w1_ref, w2_ref,
    qg_ref, kg_ref, vg_ref, w1g_ref, w2g_ref,
    att, og, w1, w2, code, gate_row, pick, slot_gate, wide,
    send_rows, send_grads, send_back, got_rows, got_grads, got_back,
    rows, grads, upper, act, upg,
    q_all, k_all, v_all, g_all, probs, sums, got_sums, inverse, delta,
    dq, dk, dv, dq_pair, dq_far, dk_far, dv_far,
    t1, t2, t1_pair, t2_pair, t1_x, t2_x, t1_z, t2_z, out1, out2,
    local_sem, out_sem, a2a_send, a2a_recv, kv_send, kv_recv, b_send, b_recv, small_send, small_recv,
    rx_send, rx_recv, rq_send, rq_recv, rz_send, rz_recv, w_send, w_recv, wx_send, wx_recv,
):
    tok, width = att.shape
    ff = act.shape[1]
    heads = width // HEAD_DIM
    cap = send_rows.shape[1]
    scale = HEAD_DIM ** (-0.5)
    me = lax.axis_index("exp")
    ctx = lax.axis_index("ctx")
    core = lax.rem(ctx, 2)
    my_x = lax.rem(ctx // 2, nx)
    zl = ctx // (2 * nx)
    b_me = zl * 2 + core

    def ctx_of(z, x, c):
        return (z * nx + x) * 2 + c

    def b_dev(b):
        return {"ctx": ctx_of(b // 2, my_x, lax.rem(b, 2))}

    def x_dev(x):
        return {"ctx": ctx_of(zl, x, core)}

    sib = {"ctx": ctx_of(zl, my_x, 1 - core)}
    zpart = {"ctx": ctx_of(1 - zl, my_x, core)}
    b_sib, b_z, b_diag = zl * 2 + 1 - core, (1 - zl) * 2 + core, (1 - zl) * 2 + 1 - core

    def remote(src, dst, ssem, rsem, dev):
        return pltpu.make_async_remote_copy(
            src_ref=src, dst_ref=dst, send_sem=ssem, recv_sem=rsem, device_id=dev, device_id_type=MESH
        )

    def blk(ref, i):
        return ref.at[pl.ds(pl.multiple_of(i * tok, tok), tok)]

    barrier = pltpu.get_barrier_semaphore()

    @pl.loop(1, nexp)
    def _(k):
        pl.semaphore_signal(barrier, inc=1, device_id={"exp": lax.rem(me + k, nexp)}, device_id_type=MESH)

    @pl.loop(1, nx)
    def _(k):
        pl.semaphore_signal(barrier, inc=1, device_id=x_dev(lax.rem(my_x + k, nx)), device_id_type=MESH)

    @pl.loop(1, 4)
    def _(k):
        pl.semaphore_signal(barrier, inc=1, device_id=b_dev(lax.rem(b_me + k, 4)), device_id_type=MESH)

    local = [
        pltpu.make_async_copy(s, d, local_sem.at[i])
        for i, (s, d) in enumerate(
            (
                (att_ref, att), (og_ref, og), (w1_ref, w1), (w2_ref, w2),
                (q_ref, blk(q_all, b_me)), (k_ref, blk(k_all, my_x)), (v_ref, blk(v_all, my_x)),
            )
        )
    ]
    for c in local:
        c.start()

    expert = lax.broadcasted_iota(jnp.int32, (nexp, tok), 0)
    first, second = ids_ref[0:1, :] == expert, ids_ref[1:2, :] == expert
    member = jnp.where(first | second, 1.0, 0.0)
    earlier = jnp.where(
        lax.broadcasted_iota(jnp.int32, (tok, tok), 0) < lax.broadcasted_iota(jnp.int32, (tok, tok), 1), 1.0, 0.0
    )
    before = dot_nn(member.astype(BF16), earlier.astype(BF16))
    code[...] = jnp.where(member > 0.5, before, -1.0)
    gate_row[...] = jnp.where(first, gates_ref[0:1, :], 0.0) + jnp.where(second, gates_ref[1:2, :], 0.0)
    slot = lax.broadcasted_iota(jnp.int32, (cap, tok), 0).astype(F32)

    @pl.loop(0, nexp)
    def _(e):
        at = pl.ds(pl.multiple_of(e * cap, 8), cap)
        here = jnp.broadcast_to(code[pl.ds(e, 1), :], (cap, tok)) == slot
        gate = jnp.broadcast_to(gate_row[pl.ds(e, 1), :], (cap, tok))
        wide[at, pl.ds(0, tok)] = jnp.where(here, 1.0, 0.0)
        slot_gate[at, :] = jnp.broadcast_to(
            jnp.sum(jnp.where(here, gate, 0.0), axis=1, keepdims=True), (cap, tok)
        )

    pick[...] = wide[:, pl.ds(0, tok)].astype(BF16)
    pl.semaphore_wait(barrier, nexp - 1 + nx - 1 + 3)

    def tiles(n, size):
        return pl.loop(0, n // size)

    def cols(j, size):
        return pl.ds(pl.multiple_of(j * size, 128), size)

    wide_tile = 256

    def dispatch(buffer, got, which):
        @pl.loop(1, nexp + 1)
        def _(k):
            e = lax.rem(me + k, nexp)
            buffer[e] = wide[pl.ds(pl.multiple_of(e * cap, 8), cap), :].astype(BF16)

            @pl.when(k < nexp)
            def _():
                remote(
                    buffer.at[e], got.at[me], a2a_send.at[which, e], a2a_recv.at[which, me], {"exp": e}
                ).start()

            @pl.when(k == nexp)
            def _():
                got[me] = buffer[me]

    def arrived(buffer, got, which):
        @pl.loop(1, nexp)
        def _(k):
            e = lax.rem(me + nexp - k, nexp)
            remote(
                buffer.at[e], got.at[e], a2a_send.at[which, e], a2a_recv.at[which, e], {"exp": e}
            ).wait_recv()

    def unpack(got, out):
        @pl.loop(0, nexp)
        def _(e):
            wide[pl.ds(pl.multiple_of(e * cap, 8), cap), :] = got[e].astype(F32)

        @tiles(width, wide_tile)
        def _(j):
            out[:, cols(j, wide_tile)] = wide[:, cols(j, wide_tile)].astype(BF16)

    local[0].wait()

    @tiles(width, wide_tile)
    def _(j):
        wide[:, cols(j, wide_tile)] = dot_nn(pick[...], att[:, cols(j, wide_tile)])

    dispatch(send_rows, got_rows, 0)
    local[1].wait()

    @tiles(width, wide_tile)
    def _(j):
        wide[:, cols(j, wide_tile)] = dot_nn(pick[...], og[:, cols(j, wide_tile)]) * slot_gate[:, 0:1]

    dispatch(send_grads, got_grads, 1)

    def b_start(src, buf, which):
        remote(src, blk(buf, b_me), b_send.at[which, 0], b_recv.at[which, 0], sib).start()
        remote(src, blk(buf, b_me), b_send.at[which, 1], b_recv.at[which, 1], zpart).start()

    def b_forward(buf, which):
        mine = blk(buf, b_z)
        remote(mine, mine, b_send.at[which, 1], b_recv.at[which, 1], zpart).wait_recv()
        remote(mine, mine, b_send.at[which, 2], b_recv.at[which, 2], sib).start()

    def b_finish(buf, which):
        s, d = blk(buf, b_sib), blk(buf, b_diag)
        remote(s, s, b_send.at[which, 0], b_recv.at[which, 0], sib).wait_recv()
        remote(d, d, b_send.at[which, 2], b_recv.at[which, 2], sib).wait_recv()

    b_start(q_ref, q_all, 0)
    for which, (src, buf) in enumerate(((k_ref, k_all), (v_ref, v_all))):
        for k in range(1, nx):
            remote(
                src, blk(buf, my_x), kv_send.at[which, k], kv_recv.at[which, k], x_dev(lax.rem(my_x + k, nx))
            ).start()

    def kv_wait(which, buf):
        for k in range(1, nx):
            x = lax.rem(my_x + nx - k, nx)
            remote(blk(buf, x), blk(buf, x), kv_send.at[which, k], kv_recv.at[which, k], x_dev(x)).wait_recv()

    b_forward(q_all, 0)
    local[4].wait()
    local[5].wait()
    local[6].wait()
    kv_wait(0, k_all)
    b_finish(q_all, 0)

    sums[...] = jnp.ones_like(sums)
    nkeys, nq = nx * tok, 4 * tok
    half = 2 * tok

    @pl.loop(0, heads)
    def _(h):
        c = cols(h, HEAD_DIM)
        qh = q_all[:, c]
        total = jnp.zeros((1, nq), F32)
        for i in range(nkeys // half):
            e = jnp.exp(dot_nt(k_all[pl.ds(i * half, half), c], qh) * scale)
            probs[h, pl.ds(i * half, half), :] = e.astype(BF16)
            total = total + jnp.sum(e, axis=0, keepdims=True)
        sums[pl.ds(h, 1), :] = total

    for k in range(1, 4):
        remote(
            sums, got_sums.at[b_me], small_send.at[0, k], small_recv.at[0, k], b_dev(lax.rem(b_me + k, 4))
        ).start()

    arrived(send_rows, got_rows, 0)
    unpack(got_rows, rows)
    local[2].wait()
    local[3].wait()
    t = min(256, ff)

    @tiles(ff, t)
    def _(j):
        upper[:, cols(j, t)] = dot_nn(rows[...], w1[:, cols(j, t)])

    arrived(send_grads, got_grads, 1)
    unpack(got_grads, grads)

    @tiles(ff, t)
    def _(j):
        u = upper[:, cols(j, t)]
        sig = jax.nn.sigmoid(u)
        act[:, cols(j, t)] = (u * sig).astype(BF16)
        back = dot_nt(grads[...], w2[cols(j, t), :])
        upg[:, cols(j, t)] = (back * sig * (1.0 + u * (1.0 - sig))).astype(BF16)

    @tiles(width, wide_tile)
    def _(j):
        wide[:, cols(j, wide_tile)] = dot_nt(upg[...], w1[cols(j, wide_tile), :])

    dispatch(send_back, got_back, 2)

    nblk = nx * 4
    wr1, wr2 = width // nblk, ff // nblk

    @pl.loop(0, 4)
    def _(j):
        term = dot_tn(rows[:, cols(j, width // 4)], upg[...]).astype(BF16)
        for i in range(nx):
            t1[i % 2, j * (nx // 2) + i // 2] = term[i * wr1 : (i + 1) * wr1]

    @pl.loop(0, 2)
    def _(j):
        term = dot_tn(act[:, cols(j, ff // 2)], grads[...]).astype(BF16)
        for i in range(2 * nx):
            t2[i % 2, j * nx + i // 2] = term[i * wr2 : (i + 1) * wr2]

    w_pair = (
        remote(t1.at[1 - core], t1_pair, w_send.at[0], w_recv.at[0], sib),
        remote(t2.at[1 - core], t2_pair, w_send.at[1], w_recv.at[1], sib),
    )
    for c in w_pair:
        c.start()
    for c in w_pair:
        c.wait()
    for i in range(2):

        @pl.loop(0, nx)
        def _(x):
            q = i * nx + x
            t1[1 - core, q] = (t1[core, q].astype(F32) + t1_pair[q].astype(F32)).astype(BF16)
            t2[1 - core, q] = (t2[core, q].astype(F32) + t2_pair[q].astype(F32)).astype(BF16)

    def w_x(k, i, to_x, dev):
        q = i * nx + to_x
        return (
            remote(t1.at[1 - core, q], t1_x.at[k, i], wx_send.at[0, k, i], wx_recv.at[0, k, i], dev),
            remote(t2.at[1 - core, q], t2_x.at[k, i], wx_send.at[1, k, i], wx_recv.at[1, k, i], dev),
        )

    for k in range(1, nx):
        x = lax.rem(my_x + k, nx)
        for i in range(2):
            for c in w_x(k, i, x, x_dev(x)):
                c.start()

    arrived(send_back, got_back, 2)
    unpack(got_back, rows)
    mine = pl.ds(pl.multiple_of(b_me * tok, tok), tok)
    ones = jnp.ones((8, HEAD_DIM), F32)

    @pl.loop(0, heads)
    def _(h):
        c = cols(h, HEAD_DIM)
        g = (og[:, c].astype(F32) + dot_tn(pick[...], rows[:, c])).astype(BF16)
        g_all[mine, c] = g
        d = lax.dot_general(
            ones, g.astype(F32) * att[:, c].astype(F32), (((1,), (1,)), ((), ())),
            preferred_element_type=F32, precision=lax.Precision.HIGHEST,
        )
        delta[b_me, pl.ds(h, 1), :] = d[0:1, :]

    b_start(blk(g_all, b_me), g_all, 1)

    def lanes(b):
        return delta.at[b]

    for k in range(1, 4):
        remote(
            lanes(b_me), lanes(b_me), small_send.at[1, k], small_recv.at[1, k], b_dev(lax.rem(b_me + k, 4))
        ).start()
    for k in range(1, 4):
        b = lax.rem(b_me + 4 - k, 4)
        remote(sums, got_sums.at[b], small_send.at[0, k], small_recv.at[0, k], b_dev(b)).wait_recv()
    got_sums[b_me] = sums[...]
    inverse[...] = 1.0 / (got_sums[0] + got_sums[1] + got_sums[2] + got_sums[3])
    kv_wait(1, v_all)
    b_forward(g_all, 1)
    for k in range(1, 4):
        b = lax.rem(b_me + 4 - k, 4)
        remote(lanes(b), lanes(b), small_send.at[1, k], small_recv.at[1, k], b_dev(b)).wait_recv()
    b_finish(g_all, 1)

    ngroup = heads // group
    gw = group * HEAD_DIM

    def part(ref, i, g):
        return ref.at[pl.ds(pl.multiple_of(i * tok, tok), tok), cols(g, gw)]

    def x_copies(g, k, to):
        return [
            remote(
                part(src, to, g), far.at[k - 1, :, cols(g, gw)], rx_send.at[w, k, g], rx_recv.at[w, k, g], x_dev(to)
            )
            for w, (src, far) in enumerate(((dk, dk_far), (dv, dv_far)))
        ]

    def pair_copies(g):
        return [
            remote(
                part(dq, i * 2 + 1 - core, g), dq_pair.at[i, :, cols(g, gw)], rq_send.at[i, g], rq_recv.at[i, g], sib
            )
            for i in range(2)
        ]

    def far_copy(g):
        return remote(part(dq, b_z, g), dq_far.at[:, cols(g, gw)], rz_send.at[g], rz_recv.at[g], zpart)

    def second_step(g):
        for c in pair_copies(g):
            c.wait_recv()
        rows_z = pl.ds(pl.multiple_of(b_z * tok, tok), tok)
        dq[rows_z, cols(g, gw)] = (
            dq[rows_z, cols(g, gw)].astype(F32) + dq_pair[1 - zl, :, cols(g, gw)].astype(F32)
        ).astype(BF16)
        far_copy(g).start()

    @pl.loop(0, ngroup)
    def _(g):
        @pl.loop(0, group)
        def _(i):
            h = g * group + i
            c = cols(h, HEAD_DIM)
            qh, gh = q_all[:, c], g_all[:, c]
            inv = inverse[pl.ds(h, 1), :]
            dl = jnp.concatenate([delta[b, pl.ds(h, 1), :] for b in range(4)], axis=1)
            q_acc = jnp.zeros((nq, HEAD_DIM), F32)
            for n in range(nkeys // half):
                r = pl.ds(n * half, half)
                kh = k_all[r, c]
                p = probs[h, r, :].astype(F32) * inv
                s = (p * (dot_nt(v_all[r, c], gh) - dl)).astype(BF16)
                dv[r, c] = dot_nn(p.astype(BF16), gh).astype(BF16)
                dk[r, c] = (dot_nn(s, qh) * scale).astype(BF16)
                q_acc = q_acc + dot_tn(s, kh)
            dq[:, c] = (q_acc * scale).astype(BF16)

        for c in pair_copies(g):
            c.start()
        for k in range(1, nx):
            for c in x_copies(g, k, lax.rem(my_x + k, nx)):
                c.start()

        @pl.when(g >= 1)
        def _():
            second_step(g - 1)

    second_step(ngroup - 1)

    for k in range(1, nx):
        for i in range(2):
            for c in w_x(k, i, my_x, x_dev(lax.rem(my_x + nx - k, nx))):
                c.wait_recv()
    for i in range(2):
        q = i * nx + my_x
        s1, s2 = t1[1 - core, q].astype(F32), t2[1 - core, q].astype(F32)
        for k in range(1, nx):
            s1, s2 = s1 + t1_x[k, i].astype(F32), s2 + t2_x[k, i].astype(F32)
        t1[core, i], t2[core, i] = s1.astype(BF16), s2.astype(BF16)
    w_z = (
        remote(t1.at[core, 1 - zl], t1_z, w_send.at[2], w_recv.at[2], zpart),
        remote(t2.at[core, 1 - zl], t2_z, w_send.at[3], w_recv.at[3], zpart),
    )
    for c in w_z:
        c.start()

    rows_x = pl.ds(pl.multiple_of(my_x * tok, tok), tok)

    @pl.loop(0, ngroup)
    def _(g):
        c = cols(g, gw)
        for k in range(1, nx):
            for d in x_copies(g, k, my_x):
                d.wait_recv()
        for src, far, out in ((dk, dk_far, 2), (dv, dv_far, 3)):
            total = src[rows_x, c].astype(F32)
            for k in range(1, nx):
                total = total + far[k - 1, :, c].astype(F32)
            src[rows_x, c] = total.astype(BF16)
        far_copy(g).wait_recv()
        dq[mine, c] = (
            dq[mine, c].astype(F32) + dq_pair[zl, :, c].astype(F32) + dq_far[:, c].astype(F32)
        ).astype(BF16)

    outs = [
        pltpu.make_async_copy(blk(dq, b_me), qg_ref, out_sem.at[0]),
        pltpu.make_async_copy(blk(dk, my_x), kg_ref, out_sem.at[1]),
        pltpu.make_async_copy(blk(dv, my_x), vg_ref, out_sem.at[2]),
    ]
    for c in outs:
        c.start()
    for c in w_z:
        c.wait()
    out1[...] = (t1[core, zl].astype(F32) + t1_z[...].astype(F32)).astype(BF16)
    out2[...] = (t2[core, zl].astype(F32) + t2_z[...].astype(F32)).astype(BF16)
    outs += [
        pltpu.make_async_copy(out1, w1g_ref, out_sem.at[3]),
        pltpu.make_async_copy(out2, w2g_ref, out_sem.at[4]),
    ]
    for c in outs[3:]:
        c.start()

    for which, buffer, got in ((0, send_rows, got_rows), (1, send_grads, got_grads), (2, send_back, got_back)):

        @pl.loop(1, nexp)
        def _(k):
            e = lax.rem(me + k, nexp)
            remote(
                buffer.at[e], got.at[me], a2a_send.at[which, e], a2a_recv.at[which, me], {"exp": e}
            ).wait_send()

    for which, src, buf in ((0, q_ref, q_all), (1, blk(g_all, b_me), g_all)):
        remote(src, blk(buf, b_me), b_send.at[which, 0], b_recv.at[which, 0], sib).wait_send()
        remote(src, blk(buf, b_me), b_send.at[which, 1], b_recv.at[which, 1], zpart).wait_send()
        z = blk(buf, b_z)
        remote(z, z, b_send.at[which, 2], b_recv.at[which, 2], sib).wait_send()
    for which, (src, buf) in enumerate(((k_ref, k_all), (v_ref, v_all))):
        for k in range(1, nx):
            remote(
                src, blk(buf, my_x), kv_send.at[which, k], kv_recv.at[which, k], x_dev(lax.rem(my_x + k, nx))
            ).wait_send()
    for k in range(1, 4):
        dev = b_dev(lax.rem(b_me + k, 4))
        remote(sums, got_sums.at[b_me], small_send.at[0, k], small_recv.at[0, k], dev).wait_send()
        remote(lanes(b_me), lanes(b_me), small_send.at[1, k], small_recv.at[1, k], dev).wait_send()
    for k in range(1, nx):
        x = lax.rem(my_x + k, nx)
        for i in range(2):
            for c in w_x(k, i, x, x_dev(x)):
                c.wait_send()

    @pl.loop(0, ngroup)
    def _(g):
        for c in pair_copies(g):
            c.wait_send()
        for k in range(1, nx):
            for c in x_copies(g, k, lax.rem(my_x + k, nx)):
                c.wait_send()
        far_copy(g).wait_send()

    for c in outs:
        c.wait()


def per_device(queries, key_states, value_states, attended, output_grad, expert_ids, gate_weights, w_in, w_out):
    tok, width = queries.shape[1:]
    ff = w_in.shape[2]
    heads = width // HEAD_DIM
    nexp, nctx = lax.axis_size("exp"), lax.axis_size("ctx")
    nx = nctx // 4
    cap = 3 * tok // nexp
    pairs = nexp * cap
    group = 3 if heads % 3 == 0 else 2
    ngroup = heads // group
    hp = -(-heads // 8) * 8
    wr1, wr2 = width // nctx, ff // nctx
    dma = pltpu.SemaphoreType.DMA
    v = pltpu.VMEM
    scratch = [
        v((tok, width), BF16), v((tok, width), BF16), v((width, ff), BF16), v((ff, width), BF16),
        v((nexp, tok), F32), v((nexp, tok), F32), v((pairs, tok), BF16), v((pairs, tok), F32), v((pairs, width), F32),
        *[v((nexp, cap, width), BF16) for _ in range(6)],
        v((pairs, width), BF16), v((pairs, width), BF16), v((pairs, ff), F32), v((pairs, ff), BF16), v((pairs, ff), BF16),
        v((4 * tok, width), BF16), v((nx * tok, width), BF16), v((nx * tok, width), BF16), v((4 * tok, width), BF16),
        v((heads, nx * tok, 4 * tok), BF16),
        v((hp, 4 * tok), F32), v((4, hp, 4 * tok), F32), v((hp, 4 * tok), F32), v((4, hp, tok), F32),
        v((4 * tok, width), BF16), v((nx * tok, width), BF16), v((nx * tok, width), BF16),
        v((2, tok, width), BF16), v((tok, width), BF16),
        v((nx - 1, tok, width), BF16), v((nx - 1, tok, width), BF16),
        v((2, 2 * nx, wr1, ff), BF16), v((2, 2 * nx, wr2, width), BF16),
        v((2 * nx, wr1, ff), BF16), v((2 * nx, wr2, width), BF16),
        v((nx, 2, wr1, ff), BF16), v((nx, 2, wr2, width), BF16),
        v((wr1, ff), BF16), v((wr2, width), BF16), v((wr1, ff), BF16), v((wr2, width), BF16),
        dma((7,)), dma((5,)), dma((3, nexp)), dma((3, nexp)), dma((2, nx)), dma((2, nx)), dma((2, 3)), dma((2, 3)),
        dma((2, 4)), dma((2, 4)), dma((2, nx, ngroup)), dma((2, nx, ngroup)), dma((2, ngroup)), dma((2, ngroup)),
        dma((ngroup,)), dma((ngroup,)), dma((4,)), dma((4,)), dma((2, nx, 2)), dma((2, nx, 2)),
    ]
    block = jax.ShapeDtypeStruct((tok, width), BF16)
    hbm = pl.BlockSpec(memory_space=pl.ANY)
    small = pl.BlockSpec(memory_space=pltpu.VMEM)
    qg, kg, vg, g1, g2 = pl.pallas_call(
        functools.partial(kernel, nx, nexp, group),
        out_shape=[
            block, block, block,
            jax.ShapeDtypeStruct((wr1, ff), BF16), jax.ShapeDtypeStruct((wr2, width), BF16),
        ],
        in_specs=[small] * 2 + [hbm] * 7,
        out_specs=[hbm] * 5,
        scratch_shapes=scratch,
        compiler_params=pltpu.CompilerParams(
            collective_id=0, has_side_effects=True, vmem_limit_bytes=60 * 1024 * 1024
        ),
        name="block_backward",
    )(
        expert_ids[0].T, gate_weights[0].T, queries[0], key_states[0], value_states[0], attended[0], output_grad[0],
        w_in[0], w_out[0],
    )
    return qg[None], kg[None], vg[None], g1[None], g2[None]


def solution(mesh):
    stream = P("exp", "ctx", None)
    return jax.shard_map(
        per_device,
        mesh=mesh,
        in_specs=(stream,) * 7 + (P("exp", None, None),) * 2,
        out_specs=(stream,) * 5,
        check_vma=False,
    )
```

```python
import functools

import jax
import jax.numpy as jnp
from jax import lax
from jax.experimental import pallas as pl
from jax.experimental.pallas import tpu as pltpu
from jax.sharding import PartitionSpec as P

HEAD_DIM = 128
MESH = pl.DeviceIdType.MESH
F32 = jnp.float32
BF16 = jnp.bfloat16
LAG = 2


def dot_nn(a, b):
    return lax.dot_general(a, b, (((1,), (0,)), ((), ())), preferred_element_type=F32)


def dot_nt(a, b):
    return lax.dot_general(a, b, (((1,), (1,)), ((), ())), preferred_element_type=F32)


def dot_tn(a, b):
    return lax.dot_general(a, b, (((0,), (0,)), ((), ())), preferred_element_type=F32)


def kernel(
    nx, ny, nexp, group,
    ids_ref, gates_ref, q_ref, k_ref, v_ref, att_ref, og_ref, w1_ref, w2_ref,
    qg_ref, kg_ref, vg_ref, w1g_ref, w2g_ref,
    att, og, w1, w2, code, gate_row, pick, pick_t, slot_gate, wide,
    send_rows, send_grads, send_back, got_rows, got_grads, got_back,
    rows, grads, upper, act, upg, stage, back,
    q_all, k_all, v_all, g_all, probs, sums, got_sums, inverse, delta,
    dq, dk, dv, dq_pair, dq_far, dk_far, dv_far, dk_relay, dv_relay,
    t1, t2, t1_pair, t2_pair, t1_x, t2_x, t1_relay, t2_relay, t1_z, t2_z, out1, out2,
    local_sem, out_sem, a2a_send, a2a_recv, back_send, back_recv, kv_send, kv_recv, q_send, q_recv, g_send, g_recv,
    sum_send, sum_recv, delta_send, delta_recv,
    rx_send, rx_recv, rq_send, rq_recv, rz_send, rz_recv, w_send, w_recv, wx_send, wx_recv,
):
    tok, width = att.shape
    ff = act.shape[1]
    heads = width // HEAD_DIM
    cap = send_rows.shape[1]
    scale = HEAD_DIM ** (-0.5)
    nz = nexp // ny
    gw = group * HEAD_DIM
    ngroup = heads // group
    me = lax.axis_index("exp")
    ctx = lax.axis_index("ctx")
    my_y, my_zh = lax.rem(me, ny), me // ny
    core = lax.rem(ctx, 2)
    my_x = lax.rem(ctx // 2, nx)
    zl = ctx // (2 * nx)
    b_me = zl * 2 + core

    def ahead(p):
        return lax.rem(my_zh + lax.rem(p, nz), nz) * ny + lax.rem(my_y + p // nz, ny)

    def behind(p):
        return lax.rem(my_zh + nz - lax.rem(p, nz), nz) * ny + lax.rem(my_y + ny - p // nz, ny)

    def ctx_of(z, x, c):
        return (z * nx + x) * 2 + c

    def b_dev(b):
        return {"ctx": ctx_of(b // 2, my_x, lax.rem(b, 2))}

    def x_dev(x):
        return {"ctx": ctx_of(zl, x, core)}

    sib = {"ctx": ctx_of(zl, my_x, 1 - core)}
    zpart = {"ctx": ctx_of(1 - zl, my_x, core)}
    b_sib, b_z, b_diag = zl * 2 + 1 - core, (1 - zl) * 2 + core, (1 - zl) * 2 + 1 - core

    def remote(src, dst, ssem, rsem, dev):
        return pltpu.make_async_remote_copy(
            src_ref=src, dst_ref=dst, send_sem=ssem, recv_sem=rsem, device_id=dev, device_id_type=MESH
        )

    def blk(ref, i):
        return ref.at[pl.ds(pl.multiple_of(i * tok, tok), tok)]

    def cols(j, size):
        return pl.ds(pl.multiple_of(j * size, 128), size)

    def part(ref, i, g):
        return ref.at[pl.ds(pl.multiple_of(i * tok, tok), tok), cols(g, gw)]

    def slots(p):
        return pl.ds(pl.multiple_of(p * cap, 8), cap)

    barrier = pltpu.get_barrier_semaphore()

    @pl.loop(1, nexp)
    def _(k):
        pl.semaphore_signal(barrier, inc=1, device_id={"exp": ahead(k)}, device_id_type=MESH)

    @pl.loop(1, nx)
    def _(k):
        pl.semaphore_signal(barrier, inc=1, device_id=x_dev(lax.rem(my_x + k, nx)), device_id_type=MESH)

    @pl.loop(1, 4)
    def _(k):
        pl.semaphore_signal(barrier, inc=1, device_id=b_dev(lax.rem(b_me + k, 4)), device_id_type=MESH)

    local = [
        pltpu.make_async_copy(s, d, local_sem.at[i])
        for i, (s, d) in enumerate(
            (
                (att_ref, att), (og_ref, og), (w1_ref, w1), (w2_ref, w2),
                (q_ref, blk(q_all, b_me)), (k_ref, blk(k_all, my_x)), (v_ref, blk(v_all, my_x)),
            )
        )
    ]
    for c in local:
        c.start()

    pl.semaphore_wait(barrier, nexp - 1 + nx - 1 + 3)
    q_sends = [
        remote(q_ref, blk(q_all, b_me), q_send.at[i], q_recv.at[i], dev) for i, dev in enumerate((sib, zpart))
    ]
    for c in q_sends:
        c.start()

    def kv_copy(which, k):
        src, buf = ((k_ref, k_all), (v_ref, v_all))[which]
        return remote(
            src, blk(buf, my_x), kv_send.at[which, k], kv_recv.at[which, k], x_dev(lax.rem(my_x + k, nx))
        )

    for which in range(2):
        for k in range(1, nx):
            kv_copy(which, k).start()
    expert = lax.broadcasted_iota(jnp.int32, (nexp, tok), 0)
    first, second = ids_ref[0:1, :] == expert, ids_ref[1:2, :] == expert
    member = jnp.where(first | second, 1.0, 0.0)
    earlier = jnp.where(
        lax.broadcasted_iota(jnp.int32, (tok, tok), 0) < lax.broadcasted_iota(jnp.int32, (tok, tok), 1), 1.0, 0.0
    )
    before = dot_nn(member.astype(BF16), earlier.astype(BF16))
    code[...] = jnp.where(member > 0.5, before, -1.0)
    gate_row[...] = jnp.where(first, gates_ref[0:1, :], 0.0) + jnp.where(second, gates_ref[1:2, :], 0.0)
    slot = lax.broadcasted_iota(jnp.int32, (cap, tok), 0).astype(F32)

    @pl.loop(0, nexp)
    def _(p):
        e = ahead(p)
        here = jnp.broadcast_to(code[pl.ds(e, 1), :], (cap, tok)) == slot
        gate = jnp.broadcast_to(gate_row[pl.ds(e, 1), :], (cap, tok))
        wide[slots(p), pl.ds(0, tok)] = jnp.where(here, 1.0, 0.0)
        slot_gate[slots(p), :] = jnp.broadcast_to(
            jnp.sum(jnp.where(here, gate, 0.0), axis=1, keepdims=True), (cap, tok)
        )

    picked = wide[:, pl.ds(0, tok)]
    pick[...] = picked.astype(BF16)
    pick_t[...] = picked.T.astype(BF16)

    def tiles(n, size):
        return pl.loop(0, n // size)

    wide_tile = 256
    nhalf = nexp // 2
    hrows = nhalf * cap

    def a2a(which, p):
        buffer, got = ((send_rows, got_rows), (send_grads, got_grads))[which]
        return remote(
            buffer.at[p], got.at[p], a2a_send.at[which, p], a2a_recv.at[which, p], {"exp": ahead(p)}
        )

    def fill(which, half):
        r = pl.ds(half * hrows, hrows)
        source, buffer = ((att, send_rows), (og, send_grads))[which]

        @tiles(width, wide_tile)
        def _(j):
            value = dot_nn(pick[r, :], source[:, cols(j, wide_tile)])
            wide[r, cols(j, wide_tile)] = value if which == 0 else value * slot_gate[r, 0:1]

        @pl.loop(half * nhalf, (half + 1) * nhalf)
        def _(p):
            buffer[p] = wide[slots(p), :].astype(BF16)

    def send(which, half):
        @pl.loop(max(1, half * nhalf), (half + 1) * nhalf)
        def _(p):
            a2a(which, p).start()

    def arrived(which, half):
        @pl.loop(max(1, half * nhalf), (half + 1) * nhalf)
        def _(p):
            a2a(which, p).wait_recv()

    local[0].wait()
    fill(0, 0)
    send(0, 0)
    local[1].wait()
    fill(1, 0)
    send(1, 0)
    fill(0, 1)
    send(0, 1)
    fill(1, 1)
    send(1, 1)
    got_rows[0] = send_rows[0]
    got_grads[0] = send_grads[0]

    def kv_wait(which, buf):
        for k in range(1, nx):
            x = lax.rem(my_x + nx - k, nx)
            remote(blk(buf, x), blk(buf, x), kv_send.at[which, k], kv_recv.at[which, k], x_dev(x)).wait_recv()

    t = min(256, ff)
    def back_copy(g, p):
        return remote(
            send_back.at[g, p], got_back.at[g, p], back_send.at[g, p], back_recv.at[g, p], {"exp": behind(p)}
        )

    def expert_half(half):
        r = pl.ds(half * hrows, hrows)

        def unpack(got, out):
            @pl.loop(half * nhalf, (half + 1) * nhalf)
            def _(p):
                wide[slots(p), :] = got[p].astype(F32)

            @tiles(width, wide_tile)
            def _(j):
                out[r, cols(j, wide_tile)] = wide[r, cols(j, wide_tile)].astype(BF16)

        arrived(0, half)
        unpack(got_rows, rows)
        if half == 0:
            local[2].wait()
            local[3].wait()

        @tiles(ff, t)
        def _(j):
            upper[:, cols(j, t)] = dot_nn(rows[r, :], w1[:, cols(j, t)])

        arrived(1, half)
        unpack(got_grads, grads)

        @tiles(ff, t)
        def _(j):
            u = upper[:, cols(j, t)]
            sig = jax.nn.sigmoid(u)
            act[r, cols(j, t)] = (u * sig).astype(BF16)
            d = dot_nt(grads[r, :], w2[cols(j, t), :])
            upg[r, cols(j, t)] = (d * sig * (1.0 + u * (1.0 - sig))).astype(BF16)

    expert_half(0)

    def q_forward():
        mine = blk(q_all, b_z)
        return remote(mine, mine, q_send.at[2], q_recv.at[2], sib)

    z, s, d = blk(q_all, b_z), blk(q_all, b_sib), blk(q_all, b_diag)
    remote(z, z, q_send.at[1], q_recv.at[1], zpart).wait_recv()
    q_forward().start()
    local[4].wait()
    local[5].wait()
    local[6].wait()
    kv_wait(0, k_all)
    remote(s, s, q_send.at[0], q_recv.at[0], sib).wait_recv()
    remote(d, d, q_send.at[2], q_recv.at[2], sib).wait_recv()
    sums[...] = jnp.ones_like(sums)
    nkeys, nq = nx * tok, 4 * tok
    part_keys = 2 * tok

    @pl.loop(0, heads)
    def _(h):
        c = cols(h, HEAD_DIM)
        qh = q_all[:, c]
        total = jnp.zeros((1, nq), F32)
        for i in range(nkeys // part_keys):
            e = jnp.exp(dot_nt(k_all[pl.ds(i * part_keys, part_keys), c], qh) * scale)
            probs[h, pl.ds(i * part_keys, part_keys), :] = e.astype(BF16)
            total = total + jnp.sum(e, axis=0, keepdims=True)
        sums[pl.ds(h, 1), :] = total

    def sum_copy(k):
        return remote(
            sums, got_sums.at[b_me], sum_send.at[k], sum_recv.at[k], b_dev(lax.rem(b_me + k, 4))
        )

    for k in range(1, 4):
        sum_copy(k).start()

    expert_half(1)

    @pl.loop(0, ngroup)
    def _(g):
        stage[...] = dot_nt(upg[...], w1[cols(g, gw), :])

        @pl.loop(0, nexp)
        def _(p):
            send_back[g, p] = stage[slots(p), :].astype(BF16)

        @pl.loop(1, nexp)
        def _(p):
            back_copy(g, p).start()

    nblk = nx * 4
    wr1, wr2 = width // nblk, ff // nblk
    x_next, x_far, x_prev = (lax.rem(my_x + k, nx) for k in range(1, 4))
    w_pair = (
        remote(t1.at[1 - core], t1_pair, w_send.at[0], w_recv.at[0], sib),
        remote(t2.at[1 - core], t2_pair, w_send.at[1], w_recv.at[1], sib),
    )

    @pl.loop(0, 4)
    def _(j):
        term = dot_tn(rows[:, cols(j, width // 4)], upg[...]).astype(BF16)
        for i in range(nx):
            t1[i % 2, j * (nx // 2) + i // 2] = term[i * wr1 : (i + 1) * wr1]

    w_pair[0].start()

    @pl.loop(0, 2)
    def _(j):
        term = dot_tn(act[:, cols(j, ff // 2)], grads[...]).astype(BF16)
        for i in range(2 * nx):
            t2[i % 2, j * nx + i // 2] = term[i * wr2 : (i + 1) * wr2]

    w_pair[1].start()

    def w_first(w):
        t, land, relay = ((t1, t1_x, t1_relay), (t2, t2_x, t2_relay))[w]
        return [
            remote(t.at[1 - core, i * nx + to], dst, wx_send.at[w, n], wx_recv.at[w, n], x_dev(dev))
            for n, (i, to, dst, dev) in enumerate(
                (
                    (0, x_far, relay.at[0], x_next), (1, x_far, relay.at[1], x_prev),
                    (1, x_next, land.at[0, 1], x_next), (0, x_prev, land.at[1, 0], x_prev),
                )
            )
        ]

    def w_second(w):
        t, land = ((t1, t1_x), (t2, t2_x))[w]
        return [
            remote(t.at[1 - core, i * nx + to], land.at[n, i], wx_send.at[w, 4 + n], wx_recv.at[w, 4 + n], x_dev(to))
            for n, (i, to) in enumerate(((0, x_next), (1, x_prev)))
        ]

    for w, (t, pair) in enumerate(((t1, t1_pair), (t2, t2_pair))):
        w_pair[w].wait()

        @pl.loop(0, 2 * nx)
        def _(q):
            t[1 - core, q] = (t[core, q].astype(F32) + pair[q].astype(F32)).astype(BF16)

        for c in w_first(w):
            c.start()

    def w_relay():
        for w, (t, relay) in enumerate(((t1, t1_relay), (t2, t2_relay))):
            for n, c in enumerate(w_first(w)[:2]):
                c.wait_recv()
                q = n * nx + (x_next, x_prev)[n]
                t[1 - core, q] = (t[1 - core, q].astype(F32) + relay[n].astype(F32)).astype(BF16)
                w_second(w)[n].start()

    w_z = (
        remote(t1.at[core, 1 - zl], t1_z, w_send.at[2], w_recv.at[2], zpart),
        remote(t2.at[core, 1 - zl], t2_z, w_send.at[3], w_recv.at[3], zpart),
    )

    def w_over_z():
        for w, (t, land) in enumerate(((t1, t1_x), (t2, t2_x))):
            for c in w_first(w)[2:] + w_second(w):
                c.wait_recv()
            for i in range(2):
                total = t[1 - core, i * nx + my_x].astype(F32) + land[0, i].astype(F32) + land[1, i].astype(F32)
                t[core, i] = total.astype(BF16)
            w_z[w].start()

    for k in range(1, 4):
        b = lax.rem(b_me + 4 - k, 4)
        remote(sums, got_sums.at[b], sum_send.at[k], sum_recv.at[k], b_dev(b)).wait_recv()
    got_sums[b_me] = sums[...]
    inverse[...] = 1.0 / (got_sums[0] + got_sums[1] + got_sums[2] + got_sums[3])
    kv_wait(1, v_all)

    mine = pl.ds(pl.multiple_of(b_me * tok, tok), tok)
    ones = jnp.ones((8, HEAD_DIM), F32)

    def g_sends(g):
        m = part(g_all, b_me, g)
        return [remote(m, m, g_send.at[i, g], g_recv.at[i, g], dev) for i, dev in enumerate((sib, zpart))]

    def g_forward(g):
        m = part(g_all, b_z, g)
        return remote(m, m, g_send.at[2, g], g_recv.at[2, g], sib)

    def delta_copy(g, k):
        m = delta.at[g, b_me]
        return remote(m, m, delta_send.at[g, k], delta_recv.at[g, k], b_dev(lax.rem(b_me + k, 4)))

    def combine(g):
        @pl.loop(1, nexp)
        def _(p):
            back_copy(g, p).wait_recv()

        stage[slots(0), :] = send_back[g, 0].astype(F32)

        @pl.loop(1, nexp)
        def _(p):
            stage[slots(p), :] = got_back[g, p].astype(F32)

        back[...] = stage[...].astype(BF16)
        c = cols(g, gw)
        total = (og[:, c].astype(F32) + dot_nn(pick_t[...], back[...])).astype(BF16)
        g_all[mine, c] = total
        for d in g_sends(g):
            d.start()
        prod = total.astype(F32) * att[:, c].astype(F32)
        for i in range(group):
            d = lax.dot_general(
                ones, prod[:, i * HEAD_DIM : (i + 1) * HEAD_DIM], (((1,), (1,)), ((), ())),
                preferred_element_type=F32, precision=lax.Precision.HIGHEST,
            )
            delta[g, b_me, i : i + 1, :] = d[0:1, :]
        for k in range(1, 4):
            delta_copy(g, k).start()

    def forward(g):
        m = part(g_all, b_z, g)
        remote(m, m, g_send.at[1, g], g_recv.at[1, g], zpart).wait_recv()
        g_forward(g).start()

    def gathered(g):
        for k in range(1, 4):
            b = lax.rem(b_me + 4 - k, 4)
            m = delta.at[g, b]
            remote(m, m, delta_send.at[g, k], delta_recv.at[g, k], b_dev(b)).wait_recv()
        m = part(g_all, b_sib, g)
        remote(m, m, g_send.at[0, g], g_recv.at[0, g], sib).wait_recv()
        m = part(g_all, b_diag, g)
        remote(m, m, g_send.at[2, g], g_recv.at[2, g], sib).wait_recv()

    half_block = tok // 2

    def half_part(ref, i, n, g):
        return ref.at[pl.ds(pl.multiple_of(i * tok + n * half_block, half_block), half_block), cols(g, gw)]

    def half_of(ref, k, n, g):
        return ref.at[k, pl.ds(n * half_block, half_block), cols(g, gw)]

    kv_parts = ((dk, dk_far, dk_relay), (dv, dv_far, dv_relay))

    def x_first(w, g):
        src, far, relay = kv_parts[w]
        return [
            remote(half_part(src, to, i, g), dst, rx_send.at[w, n, g], rx_recv.at[w, n, g], x_dev(dev))
            for n, (i, to, dst, dev) in enumerate(
                (
                    (0, x_far, relay.at[0, :, cols(g, gw)], x_next), (1, x_far, relay.at[1, :, cols(g, gw)], x_prev),
                    (1, x_next, half_of(far, 0, 1, g), x_next), (0, x_prev, half_of(far, 1, 0, g), x_prev),
                )
            )
        ]

    def x_second(w, g):
        src, far, _ = kv_parts[w]
        return [
            remote(
                half_part(src, to, n, g), half_of(far, n, n, g), rx_send.at[w, 4 + n, g], rx_recv.at[w, 4 + n, g], x_dev(to)
            )
            for n, to in enumerate((x_next, x_prev))
        ]

    def x_relay(g):
        for w, (src, _, relay) in enumerate(kv_parts):
            for n, c in enumerate(x_first(w, g)[:2]):
                c.wait_recv()
                r = pl.ds(pl.multiple_of((x_next, x_prev)[n] * tok + n * half_block, half_block), half_block)
                k = cols(g, gw)
                src[r, k] = (src[r, k].astype(F32) + relay[n, :, k].astype(F32)).astype(BF16)
                x_second(w, g)[n].start()

    def pair_copies(g):
        return [
            remote(
                part(dq, i * 2 + 1 - core, g), dq_pair.at[i, :, cols(g, gw)], rq_send.at[i, g], rq_recv.at[i, g], sib
            )
            for i in range(2)
        ]

    def far_copy(g):
        return remote(part(dq, b_z, g), dq_far.at[:, cols(g, gw)], rz_send.at[g], rz_recv.at[g], zpart)

    def attention(g):
        gathered(g)

        @pl.loop(0, group)
        def _(i):
            h = g * group + i
            c = cols(h, HEAD_DIM)
            qh, gh = q_all[:, c], g_all[:, c]
            inv = inverse[pl.ds(h, 1), :]
            dl = jnp.concatenate([delta[g, b, pl.ds(i, 1), :] for b in range(4)], axis=1)
            q_acc = jnp.zeros((nq, HEAD_DIM), F32)
            for n in range(nkeys // part_keys):
                r = pl.ds(n * part_keys, part_keys)
                kh = k_all[r, c]
                p = probs[h, r, :].astype(F32) * inv
                s = (p * (dot_nt(v_all[r, c], gh) - dl)).astype(BF16)
                dv[r, c] = dot_nn(p.astype(BF16), gh).astype(BF16)
                dk[r, c] = (dot_nn(s, qh) * scale).astype(BF16)
                q_acc = q_acc + dot_tn(s, kh)
            dq[:, c] = (q_acc * scale).astype(BF16)

        for w in range(2):
            for c in x_first(w, g):
                c.start()
        for c in pair_copies(g):
            c.start()

    def second_step(g):
        for c in pair_copies(g):
            c.wait_recv()
        rows_z = pl.ds(pl.multiple_of(b_z * tok, tok), tok)
        dq[rows_z, cols(g, gw)] = (
            dq[rows_z, cols(g, gw)].astype(F32) + dq_pair[1 - zl, :, cols(g, gw)].astype(F32)
        ).astype(BF16)
        far_copy(g).start()

    @pl.loop(0, ngroup + LAG)
    def _(step):
        @pl.when((step >= 1) & (step <= ngroup))
        def _():
            forward(step - 1)

        @pl.when(step < ngroup)
        def _():
            combine(step)

        @pl.when((step >= 1) & (step <= ngroup))
        def _():
            attention(step - 1)

        @pl.when((step >= 2) & (step < ngroup + 2))
        def _():
            second_step(step - 2)

        @pl.when(step == 1)
        def _():
            w_relay()

        @pl.when(step >= LAG)
        def _():
            x_relay(step - LAG)

        @pl.when(step == ngroup)
        def _():
            w_over_z()

    rows_x = pl.ds(pl.multiple_of(my_x * tok, tok), tok)

    @pl.loop(0, ngroup)
    def _(g):
        c = cols(g, gw)
        far_copy(g).wait_recv()
        dq[mine, c] = (
            dq[mine, c].astype(F32) + dq_pair[zl, :, c].astype(F32) + dq_far[:, c].astype(F32)
        ).astype(BF16)
        for w, (src, far, _) in enumerate(kv_parts):
            for d in x_first(w, g)[2:] + x_second(w, g):
                d.wait_recv()
            src[rows_x, c] = (
                src[rows_x, c].astype(F32) + far[0, :, c].astype(F32) + far[1, :, c].astype(F32)
            ).astype(BF16)

    outs = [
        pltpu.make_async_copy(blk(dq, b_me), qg_ref, out_sem.at[0]),
        pltpu.make_async_copy(blk(dk, my_x), kg_ref, out_sem.at[1]),
        pltpu.make_async_copy(blk(dv, my_x), vg_ref, out_sem.at[2]),
    ]
    for c in outs:
        c.start()
    for c in w_z:
        c.wait()
    out1[...] = (t1[core, zl].astype(F32) + t1_z[...].astype(F32)).astype(BF16)
    out2[...] = (t2[core, zl].astype(F32) + t2_z[...].astype(F32)).astype(BF16)
    outs += [
        pltpu.make_async_copy(out1, w1g_ref, out_sem.at[3]),
        pltpu.make_async_copy(out2, w2g_ref, out_sem.at[4]),
    ]
    for c in outs[3:]:
        c.start()

    @pl.loop(1, nexp)
    def _(p):
        a2a(0, p).wait_send()
        a2a(1, p).wait_send()

        @pl.loop(0, ngroup)
        def _(g):
            back_copy(g, p).wait_send()

    for c in q_sends:
        c.wait_send()
    q_forward().wait_send()
    for which in range(2):
        for k in range(1, nx):
            kv_copy(which, k).wait_send()
    for k in range(1, 4):
        sum_copy(k).wait_send()
    for w in range(2):
        for c in w_first(w) + w_second(w):
            c.wait_send()

    @pl.loop(0, ngroup)
    def _(g):
        for c in g_sends(g):
            c.wait_send()
        g_forward(g).wait_send()
        for k in range(1, 4):
            delta_copy(g, k).wait_send()
        for c in pair_copies(g):
            c.wait_send()
        for w in range(2):
            for c in x_first(w, g) + x_second(w, g):
                c.wait_send()
        far_copy(g).wait_send()

    for c in outs:
        c.wait()


def hand_out(*refs):
    n = len(refs) // 2
    for i in range(n):
        refs[n + i][...] = refs[i][...]


def per_device(queries, key_states, value_states, attended, output_grad, expert_ids, gate_weights, w_in, w_out):
    tok, width = queries.shape[1:]
    ff = w_in.shape[2]
    heads = width // HEAD_DIM
    nexp, nctx = lax.axis_size("exp"), lax.axis_size("ctx")
    nx, ny = nctx // 4, min(4, max(2, nexp // 4))
    cap = 3 * tok // nexp
    pairs = nexp * cap
    group = 3 if heads % 3 == 0 else 2
    ngroup, gw = heads // group, group * HEAD_DIM
    hp = -(-heads // 8) * 8
    wr1, wr2 = width // nctx, ff // nctx
    dma = pltpu.SemaphoreType.DMA
    v = pltpu.VMEM
    scratch = [
        v((tok, width), BF16), v((tok, width), BF16), v((width, ff), BF16), v((ff, width), BF16),
        v((nexp, tok), F32), v((nexp, tok), F32), v((pairs, tok), BF16), v((tok, pairs), BF16),
        v((pairs, tok), F32), v((pairs, width), F32),
        v((nexp, cap, width), BF16), v((nexp, cap, width), BF16), v((ngroup, nexp, cap, gw), BF16),
        v((nexp, cap, width), BF16), v((nexp, cap, width), BF16), v((ngroup, nexp, cap, gw), BF16),
        v((pairs, width), BF16), v((pairs, width), BF16), v((pairs // 2, ff), F32), v((pairs, ff), BF16), v((pairs, ff), BF16),
        v((pairs, gw), F32), v((pairs, gw), BF16),
        v((4 * tok, width), BF16), v((nx * tok, width), BF16), v((nx * tok, width), BF16), v((4 * tok, width), BF16),
        v((heads, nx * tok, 4 * tok), BF16),
        v((hp, 4 * tok), F32), v((4, hp, 4 * tok), F32), v((hp, 4 * tok), F32), v((ngroup, 4, 8, tok), F32),
        v((4 * tok, width), BF16), v((nx * tok, width), BF16), v((nx * tok, width), BF16),
        v((2, tok, width), BF16), v((tok, width), BF16),
        v((2, tok, width), BF16), v((2, tok, width), BF16),
        v((2, tok // 2, width), BF16), v((2, tok // 2, width), BF16),
        v((2, 2 * nx, wr1, ff), BF16), v((2, 2 * nx, wr2, width), BF16),
        v((2 * nx, wr1, ff), BF16), v((2 * nx, wr2, width), BF16),
        v((2, 2, wr1, ff), BF16), v((2, 2, wr2, width), BF16), v((2, wr1, ff), BF16), v((2, wr2, width), BF16),
        v((wr1, ff), BF16), v((wr2, width), BF16), v((wr1, ff), BF16), v((wr2, width), BF16),
        dma((7,)), dma((5,)), dma((2, nexp)), dma((2, nexp)), dma((ngroup, nexp)), dma((ngroup, nexp)), dma((2, nx)), dma((2, nx)),
        dma((3,)), dma((3,)), dma((3, ngroup)), dma((3, ngroup)), dma((4,)), dma((4,)), dma((ngroup, 4)), dma((ngroup, 4)),
        dma((2, 6, ngroup)), dma((2, 6, ngroup)), dma((2, ngroup)), dma((2, ngroup)),
        dma((ngroup,)), dma((ngroup,)), dma((4,)), dma((4,)), dma((2, 6)), dma((2, 6)),
    ]
    block = jax.ShapeDtypeStruct((tok, width), BF16)
    shapes = [block, block, block, jax.ShapeDtypeStruct((wr1, ff), BF16), jax.ShapeDtypeStruct((wr2, width), BF16)]
    hbm = pl.BlockSpec(memory_space=pl.ANY)
    small = pl.BlockSpec(memory_space=pltpu.VMEM)
    results = pl.pallas_call(
        functools.partial(kernel, nx, ny, nexp, group),
        out_shape=shapes,
        in_specs=[small] * 2 + [hbm] * 7,
        out_specs=[hbm] * 5,
        scratch_shapes=scratch,
        compiler_params=pltpu.CompilerParams(
            collective_id=0, has_side_effects=True, vmem_limit_bytes=60 * 1024 * 1024
        ),
        name="block_backward",
    )(
        expert_ids[0].T, gate_weights[0].T, queries[0], key_states[0], value_states[0], attended[0], output_grad[0],
        w_in[0], w_out[0],
    )
    results = pl.pallas_call(
        hand_out, out_shape=shapes, in_specs=[small] * 5, out_specs=[small] * 5, name="hand_out"
    )(*results)
    return tuple(r[None] for r in results)


def solution(mesh):
    stream = P("exp", "ctx", None)
    return jax.shard_map(
        per_device,
        mesh=mesh,
        in_specs=(stream,) * 7 + (P("exp", None, None),) * 2,
        out_specs=(stream,) * 5,
        check_vma=False,
    )
```

```python
import functools

import jax
import jax.numpy as jnp
from jax import lax
from jax.experimental import pallas as pl
from jax.experimental.pallas import tpu as pltpu
from jax.sharding import PartitionSpec as P

HEAD_DIM = 128
MESH = pl.DeviceIdType.MESH
F32 = jnp.float32
BF16 = jnp.bfloat16
LAG = 2
AHEAD = 2


def dot_nn(a, b):
    return lax.dot_general(a, b, (((1,), (0,)), ((), ())), preferred_element_type=F32)


def dot_nt(a, b):
    return lax.dot_general(a, b, (((1,), (1,)), ((), ())), preferred_element_type=F32)


def dot_tn(a, b):
    return lax.dot_general(a, b, (((0,), (0,)), ((), ())), preferred_element_type=F32)


def kernel(
    nx, ny, nexp, group,
    ids_ref, gates_ref, q_ref, k_ref, v_ref, att_ref, og_ref, w1_ref, w2_ref,
    qg_ref, kg_ref, vg_ref, w1g_ref, w2g_ref,
    att, og, w1, w2, code, gate_row, pick, pick_t, slot_gate, wide,
    send_rows, send_grads, send_back, got_rows, got_grads, got_back,
    rows, grads, upper, act, upg, stage, back,
    q_all, k_all, v_all, g_all, probs, sums, got_sums, inverse, delta,
    dq, dk, dv, dq_pair, dq_far, dk_far, dv_far, dk_relay, dv_relay,
    t1, t2, t1_pair, t2_pair, t1_x, t2_x, t1_relay, t2_relay, t1_z, t2_z, out1, out2,
    local_sem, out_sem, a2a_send, a2a_recv, back_send, back_recv, kv_send, kv_recv, q_send, q_recv, g_send, g_recv,
    sum_send, sum_recv, delta_send, delta_recv,
    rx_send, rx_recv, rq_send, rq_recv, rz_send, rz_recv, w_send, w_recv, wx_send, wx_recv,
):
    tok, width = att.shape
    ff = act.shape[1]
    heads = width // HEAD_DIM
    cap = send_rows.shape[1]
    scale = HEAD_DIM ** (-0.5)
    nz = nexp // ny
    gw = group * HEAD_DIM
    ngroup = heads // group
    me = lax.axis_index("exp")
    ctx = lax.axis_index("ctx")
    my_y, my_zh = lax.rem(me, ny), me // ny
    core = lax.rem(ctx, 2)
    my_x = lax.rem(ctx // 2, nx)
    zl = ctx // (2 * nx)
    b_me = zl * 2 + core

    place = ((zl, 0), (0, 1 + zl), (1 - zl, 3), (1, 1 + zl))
    origin = ((0, zl), (1 + 2 * zl, 0), (1 + 2 * zl, 1), (2, 1 - zl))

    def owner(dy, s):
        return lax.rem(my_zh + s, nz) * ny + lax.rem(my_y + dy, ny)

    def worker(dy, s):
        return {"exp": owner(dy, s), "ctx": ctx_of(place[s][0], my_x, core)}

    def source(dy, r):
        s, z = origin[r]
        return {
            "exp": lax.rem(my_zh + nz - s, nz) * ny + lax.rem(my_y + ny - dy, ny), "ctx": ctx_of(z, my_x, core)
        }

    def chunks(first, last, body):
        @pl.loop(first, last)
        def _(dy):
            for n in range(nz):
                if n == 0:
                    pl.when(dy > 0)(functools.partial(body, dy, n))
                else:
                    body(dy, n)

    def ctx_of(z, x, c):
        return (z * nx + x) * 2 + c

    def b_dev(b):
        return {"ctx": ctx_of(b // 2, my_x, lax.rem(b, 2))}

    def x_dev(x):
        return {"ctx": ctx_of(zl, x, core)}

    sib = {"ctx": ctx_of(zl, my_x, 1 - core)}
    zpart = {"ctx": ctx_of(1 - zl, my_x, core)}
    b_sib, b_z, b_diag = zl * 2 + 1 - core, (1 - zl) * 2 + core, (1 - zl) * 2 + 1 - core

    def remote(src, dst, ssem, rsem, dev):
        return pltpu.make_async_remote_copy(
            src_ref=src, dst_ref=dst, send_sem=ssem, recv_sem=rsem, device_id=dev, device_id_type=MESH
        )

    def blk(ref, i):
        return ref.at[pl.ds(pl.multiple_of(i * tok, tok), tok)]

    def cols(j, size):
        return pl.ds(pl.multiple_of(j * size, 128), size)

    def part(ref, i, g):
        return ref.at[pl.ds(pl.multiple_of(i * tok, tok), tok), cols(g, gw)]

    def slots(p):
        return pl.ds(pl.multiple_of(p * cap, 8), cap)

    barrier = pltpu.get_barrier_semaphore()

    def greet(dy, n):
        for dev in (worker(dy, n), source(dy, n)):
            pl.semaphore_signal(barrier, inc=1, device_id=dev, device_id_type=MESH)

    chunks(0, ny, greet)

    @pl.loop(1, nx)
    def _(k):
        pl.semaphore_signal(barrier, inc=1, device_id=x_dev(lax.rem(my_x + k, nx)), device_id_type=MESH)

    @pl.loop(1, 4)
    def _(k):
        pl.semaphore_signal(barrier, inc=1, device_id=b_dev(lax.rem(b_me + k, 4)), device_id_type=MESH)

    local = [
        pltpu.make_async_copy(s, d, local_sem.at[i])
        for i, (s, d) in enumerate(
            (
                (att_ref, att), (og_ref, og), (w1_ref, w1), (w2_ref, w2),
                (q_ref, blk(q_all, b_me)), (k_ref, blk(k_all, my_x)), (v_ref, blk(v_all, my_x)),
            )
        )
    ]
    for c in local:
        c.start()

    pl.semaphore_wait(barrier, 2 * (nexp - 1) + nx - 1 + 3)
    q_sends = [
        remote(q_ref, blk(q_all, b_me), q_send.at[i], q_recv.at[i], dev) for i, dev in enumerate((sib, zpart))
    ]
    for c in q_sends:
        c.start()

    def kv_copy(which, k):
        src, buf = ((k_ref, k_all), (v_ref, v_all))[which]
        return remote(
            src, blk(buf, my_x), kv_send.at[which, k], kv_recv.at[which, k], x_dev(lax.rem(my_x + k, nx))
        )

    for k in range(1, nx):
        kv_copy(0, k).start()
    expert = lax.broadcasted_iota(jnp.int32, (nexp, tok), 0)
    first, second = ids_ref[0:1, :] == expert, ids_ref[1:2, :] == expert
    member = jnp.where(first | second, 1.0, 0.0)
    earlier = jnp.where(
        lax.broadcasted_iota(jnp.int32, (tok, tok), 0) < lax.broadcasted_iota(jnp.int32, (tok, tok), 1), 1.0, 0.0
    )
    before = dot_nn(member.astype(BF16), earlier.astype(BF16))
    code[...] = jnp.where(member > 0.5, before, -1.0)
    gate_row[...] = jnp.where(first, gates_ref[0:1, :], 0.0) + jnp.where(second, gates_ref[1:2, :], 0.0)
    slot = lax.broadcasted_iota(jnp.int32, (cap, tok), 0).astype(F32)

    @pl.loop(0, nexp)
    def _(p):
        e = owner(p // nz, lax.rem(p, nz))
        here = jnp.broadcast_to(code[pl.ds(e, 1), :], (cap, tok)) == slot
        gate = jnp.broadcast_to(gate_row[pl.ds(e, 1), :], (cap, tok))
        wide[slots(p), pl.ds(0, tok)] = jnp.where(here, 1.0, 0.0)
        slot_gate[slots(p), :] = jnp.broadcast_to(
            jnp.sum(jnp.where(here, gate, 0.0), axis=1, keepdims=True), (cap, tok)
        )

    picked = wide[:, pl.ds(0, tok)]
    pick[...] = picked.astype(BF16)
    pick_t[...] = picked.T.astype(BF16)

    def tiles(n, size):
        return pl.loop(0, n // size)

    wide_tile = 256
    nhalf = nexp // 2
    hrows = nhalf * cap

    hy = ny // 2

    def a2a(which, dy, s):
        buffer, got = ((send_rows, got_rows), (send_grads, got_grads))[which]
        here, there = dy * nz + s, dy * nz + place[s][1]
        return remote(
            buffer.at[here], got.at[there], a2a_send.at[which, here], a2a_recv.at[which, there], worker(dy, s)
        )

    def fill(which, half):
        r = pl.ds(half * hrows, hrows)
        source, buffer = ((att, send_rows), (og, send_grads))[which]

        @tiles(width, wide_tile)
        def _(j):
            value = dot_nn(pick[r, :], source[:, cols(j, wide_tile)])
            wide[r, cols(j, wide_tile)] = value if which == 0 else value * slot_gate[r, 0:1]

        @pl.loop(half * nhalf, (half + 1) * nhalf)
        def _(p):
            buffer[p] = wide[slots(p), :].astype(BF16)

    def send(which, half):
        chunks(half * hy, (half + 1) * hy, lambda dy, s: a2a(which, dy, s).start())

    def arrived(which, half):
        buffer, got = ((send_rows, got_rows), (send_grads, got_grads))[which]

        def wait(dy, r):
            p = dy * nz + r
            remote(buffer.at[p], got.at[p], a2a_send.at[which, p], a2a_recv.at[which, p], source(dy, r)).wait_recv()

        chunks(half * hy, (half + 1) * hy, wait)

    local[0].wait()
    fill(0, 0)
    send(0, 0)
    local[1].wait()
    fill(1, 0)
    send(1, 0)
    fill(0, 1)
    send(0, 1)
    fill(1, 1)
    send(1, 1)
    for k in range(1, nx):
        kv_copy(1, k).start()
    got_rows[0] = send_rows[0]
    got_grads[0] = send_grads[0]

    def kv_wait(which, buf):
        for k in range(1, nx):
            x = lax.rem(my_x + nx - k, nx)
            remote(blk(buf, x), blk(buf, x), kv_send.at[which, k], kv_recv.at[which, k], x_dev(x)).wait_recv()

    t = min(256, ff)
    def back_copy(g, dy, r):
        here, there = dy * nz + r, dy * nz + origin[r][0]
        return remote(
            send_back.at[g, here], got_back.at[g, there], back_send.at[g, here], back_recv.at[g, there], source(dy, r)
        )

    def back_wait(g, dy, s):
        p = dy * nz + s
        remote(
            send_back.at[g, p], got_back.at[g, p], back_send.at[g, p], back_recv.at[g, p], worker(dy, s)
        ).wait_recv()

    def expert_half(half):
        r = pl.ds(half * hrows, hrows)

        def unpack(got, out):
            @pl.loop(half * nhalf, (half + 1) * nhalf)
            def _(p):
                wide[slots(p), :] = got[p].astype(F32)

            @tiles(width, wide_tile)
            def _(j):
                out[r, cols(j, wide_tile)] = wide[r, cols(j, wide_tile)].astype(BF16)

        arrived(0, half)
        unpack(got_rows, rows)
        if half == 0:
            local[2].wait()
            local[3].wait()

        @tiles(ff, t)
        def _(j):
            upper[:, cols(j, t)] = dot_nn(rows[r, :], w1[:, cols(j, t)])

        arrived(1, half)
        unpack(got_grads, grads)

        @tiles(ff, t)
        def _(j):
            u = upper[:, cols(j, t)]
            sig = jax.nn.sigmoid(u)
            act[r, cols(j, t)] = (u * sig).astype(BF16)
            d = dot_nt(grads[r, :], w2[cols(j, t), :])
            upg[r, cols(j, t)] = (d * sig * (1.0 + u * (1.0 - sig))).astype(BF16)

    expert_half(0)

    def q_forward():
        mine = blk(q_all, b_z)
        return remote(mine, mine, q_send.at[2], q_recv.at[2], sib)

    z, s, d = blk(q_all, b_z), blk(q_all, b_sib), blk(q_all, b_diag)
    remote(z, z, q_send.at[1], q_recv.at[1], zpart).wait_recv()
    q_forward().start()
    local[4].wait()
    local[5].wait()
    local[6].wait()
    kv_wait(0, k_all)
    remote(s, s, q_send.at[0], q_recv.at[0], sib).wait_recv()
    remote(d, d, q_send.at[2], q_recv.at[2], sib).wait_recv()
    sums[...] = jnp.ones_like(sums)
    nkeys, nq = nx * tok, 4 * tok
    part_keys = 2 * tok

    @pl.loop(0, heads)
    def _(h):
        c = cols(h, HEAD_DIM)
        qh = q_all[:, c]
        total = jnp.zeros((1, nq), F32)
        for i in range(nkeys // part_keys):
            e = jnp.exp(dot_nt(k_all[pl.ds(i * part_keys, part_keys), c], qh) * scale)
            probs[h, pl.ds(i * part_keys, part_keys), :] = e.astype(BF16)
            total = total + jnp.sum(e, axis=0, keepdims=True)
        sums[pl.ds(h, 1), :] = total

    def sum_copy(k):
        return remote(
            sums, got_sums.at[b_me], sum_send.at[k], sum_recv.at[k], b_dev(lax.rem(b_me + k, 4))
        )

    for k in range(1, 4):
        sum_copy(k).start()

    expert_half(1)

    def return_group(g):
        chunks(0, ny, lambda dy, r: back_copy(g, dy, r).start())

    @pl.loop(0, ngroup)
    def _(g):
        stage[...] = dot_nt(upg[...], w1[cols(g, gw), :])

        @pl.loop(0, nexp)
        def _(p):
            send_back[g, p] = stage[slots(p), :].astype(BF16)

        @pl.when(g < AHEAD)
        def _():
            return_group(g)

    nblk = nx * 4
    wr1, wr2 = width // nblk, ff // nblk
    x_next, x_far, x_prev = (lax.rem(my_x + k, nx) for k in range(1, 4))
    w_pair = (
        remote(t1.at[1 - core], t1_pair, w_send.at[0], w_recv.at[0], sib),
        remote(t2.at[1 - core], t2_pair, w_send.at[1], w_recv.at[1], sib),
    )

    @pl.loop(0, 4)
    def _(j):
        term = dot_tn(rows[:, cols(j, width // 4)], upg[...]).astype(BF16)
        for i in range(nx):
            t1[i % 2, j * (nx // 2) + i // 2] = term[i * wr1 : (i + 1) * wr1]

    w_pair[0].start()

    @pl.loop(0, 2)
    def _(j):
        term = dot_tn(act[:, cols(j, ff // 2)], grads[...]).astype(BF16)
        for i in range(2 * nx):
            t2[i % 2, j * nx + i // 2] = term[i * wr2 : (i + 1) * wr2]

    w_pair[1].start()

    def w_first(w):
        t, land, relay = ((t1, t1_x, t1_relay), (t2, t2_x, t2_relay))[w]
        return [
            remote(t.at[1 - core, i * nx + to], dst, wx_send.at[w, n], wx_recv.at[w, n], x_dev(dev))
            for n, (i, to, dst, dev) in enumerate(
                (
                    (0, x_far, relay.at[0], x_next), (1, x_far, relay.at[1], x_prev),
                    (1, x_next, land.at[0, 1], x_next), (0, x_prev, land.at[1, 0], x_prev),
                )
            )
        ]

    def w_second(w):
        t, land = ((t1, t1_x), (t2, t2_x))[w]
        return [
            remote(t.at[1 - core, i * nx + to], land.at[n, i], wx_send.at[w, 4 + n], wx_recv.at[w, 4 + n], x_dev(to))
            for n, (i, to) in enumerate(((0, x_next), (1, x_prev)))
        ]

    for w, (t, pair) in enumerate(((t1, t1_pair), (t2, t2_pair))):
        w_pair[w].wait()

        @pl.loop(0, 2 * nx)
        def _(q):
            t[1 - core, q] = (t[core, q].astype(F32) + pair[q].astype(F32)).astype(BF16)

        for c in w_first(w):
            c.start()

    def w_relay():
        for w, (t, relay) in enumerate(((t1, t1_relay), (t2, t2_relay))):
            for n, c in enumerate(w_first(w)[:2]):
                c.wait_recv()
                q = n * nx + (x_next, x_prev)[n]
                t[1 - core, q] = (t[1 - core, q].astype(F32) + relay[n].astype(F32)).astype(BF16)
                w_second(w)[n].start()

    w_z = (
        remote(t1.at[core, 1 - zl], t1_z, w_send.at[2], w_recv.at[2], zpart),
        remote(t2.at[core, 1 - zl], t2_z, w_send.at[3], w_recv.at[3], zpart),
    )

    def w_over_z():
        for w, (t, land) in enumerate(((t1, t1_x), (t2, t2_x))):
            for c in w_first(w)[2:] + w_second(w):
                c.wait_recv()
            for i in range(2):
                total = t[1 - core, i * nx + my_x].astype(F32) + land[0, i].astype(F32) + land[1, i].astype(F32)
                t[core, i] = total.astype(BF16)
            w_z[w].start()

    for k in range(1, 4):
        b = lax.rem(b_me + 4 - k, 4)
        remote(sums, got_sums.at[b], sum_send.at[k], sum_recv.at[k], b_dev(b)).wait_recv()
    got_sums[b_me] = sums[...]
    inverse[...] = 1.0 / (got_sums[0] + got_sums[1] + got_sums[2] + got_sums[3])
    kv_wait(1, v_all)

    mine = pl.ds(pl.multiple_of(b_me * tok, tok), tok)
    ones = jnp.ones((8, HEAD_DIM), F32)

    def g_sends(g):
        m = part(g_all, b_me, g)
        return [remote(m, m, g_send.at[i, g], g_recv.at[i, g], dev) for i, dev in enumerate((sib, zpart))]

    def g_forward(g):
        m = part(g_all, b_z, g)
        return remote(m, m, g_send.at[2, g], g_recv.at[2, g], sib)

    def delta_copy(g, k):
        m = delta.at[g, b_me]
        return remote(m, m, delta_send.at[g, k], delta_recv.at[g, k], b_dev(lax.rem(b_me + k, 4)))

    def combine(g):
        chunks(0, ny, functools.partial(back_wait, g))

        stage[slots(0), :] = send_back[g, 0].astype(F32)

        @pl.loop(1, nexp)
        def _(p):
            stage[slots(p), :] = got_back[g, p].astype(F32)

        back[...] = stage[...].astype(BF16)
        c = cols(g, gw)
        total = (og[:, c].astype(F32) + dot_nn(pick_t[...], back[...])).astype(BF16)
        g_all[mine, c] = total
        for d in g_sends(g):
            d.start()

        @pl.when(g + AHEAD < ngroup)
        def _():
            return_group(g + AHEAD)

        prod = total.astype(F32) * att[:, c].astype(F32)
        for i in range(group):
            d = lax.dot_general(
                ones, prod[:, i * HEAD_DIM : (i + 1) * HEAD_DIM], (((1,), (1,)), ((), ())),
                preferred_element_type=F32, precision=lax.Precision.HIGHEST,
            )
            delta[g, b_me, i : i + 1, :] = d[0:1, :]
        for k in range(1, 4):
            delta_copy(g, k).start()

    def forward(g):
        m = part(g_all, b_z, g)
        remote(m, m, g_send.at[1, g], g_recv.at[1, g], zpart).wait_recv()
        g_forward(g).start()

    def gathered(g):
        for k in range(1, 4):
            b = lax.rem(b_me + 4 - k, 4)
            m = delta.at[g, b]
            remote(m, m, delta_send.at[g, k], delta_recv.at[g, k], b_dev(b)).wait_recv()
        m = part(g_all, b_sib, g)
        remote(m, m, g_send.at[0, g], g_recv.at[0, g], sib).wait_recv()
        m = part(g_all, b_diag, g)
        remote(m, m, g_send.at[2, g], g_recv.at[2, g], sib).wait_recv()

    half_block = tok // 2

    def half_part(ref, i, n, g):
        return ref.at[pl.ds(pl.multiple_of(i * tok + n * half_block, half_block), half_block), cols(g, gw)]

    def half_of(ref, k, n, g):
        return ref.at[k, pl.ds(n * half_block, half_block), cols(g, gw)]

    kv_parts = ((dk, dk_far, dk_relay), (dv, dv_far, dv_relay))

    def x_first(w, g):
        src, far, relay = kv_parts[w]
        return [
            remote(half_part(src, to, i, g), dst, rx_send.at[w, n, g], rx_recv.at[w, n, g], x_dev(dev))
            for n, (i, to, dst, dev) in enumerate(
                (
                    (0, x_far, relay.at[0, :, cols(g, gw)], x_next), (1, x_far, relay.at[1, :, cols(g, gw)], x_prev),
                    (1, x_next, half_of(far, 0, 1, g), x_next), (0, x_prev, half_of(far, 1, 0, g), x_prev),
                )
            )
        ]

    def x_second(w, g):
        src, far, _ = kv_parts[w]
        return [
            remote(
                half_part(src, to, n, g), half_of(far, n, n, g), rx_send.at[w, 4 + n, g], rx_recv.at[w, 4 + n, g], x_dev(to)
            )
            for n, to in enumerate((x_next, x_prev))
        ]

    def x_relay(g):
        for w, (src, _, relay) in enumerate(kv_parts):
            for n, c in enumerate(x_first(w, g)[:2]):
                c.wait_recv()
                r = pl.ds(pl.multiple_of((x_next, x_prev)[n] * tok + n * half_block, half_block), half_block)
                k = cols(g, gw)
                src[r, k] = (src[r, k].astype(F32) + relay[n, :, k].astype(F32)).astype(BF16)
                x_second(w, g)[n].start()

    def pair_copies(g):
        return [
            remote(
                part(dq, i * 2 + 1 - core, g), dq_pair.at[i, :, cols(g, gw)], rq_send.at[i, g], rq_recv.at[i, g], sib
            )
            for i in range(2)
        ]

    def far_copy(g):
        return remote(part(dq, b_z, g), dq_far.at[:, cols(g, gw)], rz_send.at[g], rz_recv.at[g], zpart)

    def attention(g):
        gathered(g)

        @pl.loop(0, group)
        def _(i):
            h = g * group + i
            c = cols(h, HEAD_DIM)
            qh, gh = q_all[:, c], g_all[:, c]
            inv = inverse[pl.ds(h, 1), :]
            dl = jnp.concatenate([delta[g, b, pl.ds(i, 1), :] for b in range(4)], axis=1)
            q_acc = jnp.zeros((nq, HEAD_DIM), F32)
            for n in range(nkeys // part_keys):
                r = pl.ds(n * part_keys, part_keys)
                kh = k_all[r, c]
                p = probs[h, r, :].astype(F32) * inv
                s = (p * (dot_nt(v_all[r, c], gh) - dl)).astype(BF16)
                dv[r, c] = dot_nn(p.astype(BF16), gh).astype(BF16)
                dk[r, c] = (dot_nn(s, qh) * scale).astype(BF16)
                q_acc = q_acc + dot_tn(s, kh)
            dq[:, c] = (q_acc * scale).astype(BF16)

        for w in range(2):
            for c in x_first(w, g):
                c.start()
        for c in pair_copies(g):
            c.start()

    def second_step(g):
        for c in pair_copies(g):
            c.wait_recv()
        rows_z = pl.ds(pl.multiple_of(b_z * tok, tok), tok)
        dq[rows_z, cols(g, gw)] = (
            dq[rows_z, cols(g, gw)].astype(F32) + dq_pair[1 - zl, :, cols(g, gw)].astype(F32)
        ).astype(BF16)
        far_copy(g).start()

    @pl.loop(0, ngroup + LAG)
    def _(step):
        @pl.when((step >= 1) & (step <= ngroup))
        def _():
            forward(step - 1)

        @pl.when(step < ngroup)
        def _():
            combine(step)

        @pl.when((step >= 1) & (step <= ngroup))
        def _():
            attention(step - 1)

        @pl.when((step >= 2) & (step < ngroup + 2))
        def _():
            second_step(step - 2)

        @pl.when(step == 1)
        def _():
            w_relay()

        @pl.when(step >= LAG)
        def _():
            x_relay(step - LAG)

        @pl.when(step == ngroup)
        def _():
            w_over_z()

    rows_x = pl.ds(pl.multiple_of(my_x * tok, tok), tok)

    @pl.loop(0, ngroup)
    def _(g):
        c = cols(g, gw)
        far_copy(g).wait_recv()
        dq[mine, c] = (
            dq[mine, c].astype(F32) + dq_pair[zl, :, c].astype(F32) + dq_far[:, c].astype(F32)
        ).astype(BF16)
        for w, (src, far, _) in enumerate(kv_parts):
            for d in x_first(w, g)[2:] + x_second(w, g):
                d.wait_recv()
            src[rows_x, c] = (
                src[rows_x, c].astype(F32) + far[0, :, c].astype(F32) + far[1, :, c].astype(F32)
            ).astype(BF16)

    outs = [
        pltpu.make_async_copy(blk(dq, b_me), qg_ref, out_sem.at[0]),
        pltpu.make_async_copy(blk(dk, my_x), kg_ref, out_sem.at[1]),
        pltpu.make_async_copy(blk(dv, my_x), vg_ref, out_sem.at[2]),
    ]
    for c in outs:
        c.start()
    for c in w_z:
        c.wait()
    out1[...] = (t1[core, zl].astype(F32) + t1_z[...].astype(F32)).astype(BF16)
    out2[...] = (t2[core, zl].astype(F32) + t2_z[...].astype(F32)).astype(BF16)
    outs += [
        pltpu.make_async_copy(out1, w1g_ref, out_sem.at[3]),
        pltpu.make_async_copy(out2, w2g_ref, out_sem.at[4]),
    ]
    for c in outs[3:]:
        c.start()

    def sent(dy, n):
        a2a(0, dy, n).wait_send()
        a2a(1, dy, n).wait_send()

        @pl.loop(0, ngroup)
        def _(g):
            back_copy(g, dy, n).wait_send()

    chunks(0, ny, sent)

    for c in q_sends:
        c.wait_send()
    q_forward().wait_send()
    for which in range(2):
        for k in range(1, nx):
            kv_copy(which, k).wait_send()
    for k in range(1, 4):
        sum_copy(k).wait_send()
    for w in range(2):
        for c in w_first(w) + w_second(w):
            c.wait_send()

    @pl.loop(0, ngroup)
    def _(g):
        for c in g_sends(g):
            c.wait_send()
        g_forward(g).wait_send()
        for k in range(1, 4):
            delta_copy(g, k).wait_send()
        for c in pair_copies(g):
            c.wait_send()
        for w in range(2):
            for c in x_first(w, g) + x_second(w, g):
                c.wait_send()
        far_copy(g).wait_send()

    for c in outs:
        c.wait()


def hand_out(*refs):
    n = len(refs) // 2
    for i in range(n):
        refs[n + i][...] = refs[i][...]


def per_device(queries, key_states, value_states, attended, output_grad, expert_ids, gate_weights, w_in, w_out):
    tok, width = queries.shape[1:]
    ff = w_in.shape[2]
    heads = width // HEAD_DIM
    nexp, nctx = lax.axis_size("exp"), lax.axis_size("ctx")
    nx, ny = nctx // 4, nexp // 4
    cap = 3 * tok // nexp
    pairs = nexp * cap
    group = 3 if heads % 3 == 0 else 2
    ngroup, gw = heads // group, group * HEAD_DIM
    hp = -(-heads // 8) * 8
    wr1, wr2 = width // nctx, ff // nctx
    dma = pltpu.SemaphoreType.DMA
    v = pltpu.VMEM
    scratch = [
        v((tok, width), BF16), v((tok, width), BF16), v((width, ff), BF16), v((ff, width), BF16),
        v((nexp, tok), F32), v((nexp, tok), F32), v((pairs, tok), BF16), v((tok, pairs), BF16),
        v((pairs, tok), F32), v((pairs, width), F32),
        v((nexp, cap, width), BF16), v((nexp, cap, width), BF16), v((ngroup, nexp, cap, gw), BF16),
        v((nexp, cap, width), BF16), v((nexp, cap, width), BF16), v((ngroup, nexp, cap, gw), BF16),
        v((pairs, width), BF16), v((pairs, width), BF16), v((pairs // 2, ff), F32), v((pairs, ff), BF16), v((pairs, ff), BF16),
        v((pairs, gw), F32), v((pairs, gw), BF16),
        v((4 * tok, width), BF16), v((nx * tok, width), BF16), v((nx * tok, width), BF16), v((4 * tok, width), BF16),
        v((heads, nx * tok, 4 * tok), BF16),
        v((hp, 4 * tok), F32), v((4, hp, 4 * tok), F32), v((hp, 4 * tok), F32), v((ngroup, 4, 8, tok), F32),
        v((4 * tok, width), BF16), v((nx * tok, width), BF16), v((nx * tok, width), BF16),
        v((2, tok, width), BF16), v((tok, width), BF16),
        v((2, tok, width), BF16), v((2, tok, width), BF16),
        v((2, tok // 2, width), BF16), v((2, tok // 2, width), BF16),
        v((2, 2 * nx, wr1, ff), BF16), v((2, 2 * nx, wr2, width), BF16),
        v((2 * nx, wr1, ff), BF16), v((2 * nx, wr2, width), BF16),
        v((2, 2, wr1, ff), BF16), v((2, 2, wr2, width), BF16), v((2, wr1, ff), BF16), v((2, wr2, width), BF16),
        v((wr1, ff), BF16), v((wr2, width), BF16), v((wr1, ff), BF16), v((wr2, width), BF16),
        dma((7,)), dma((5,)), dma((2, nexp)), dma((2, nexp)), dma((ngroup, nexp)), dma((ngroup, nexp)), dma((2, nx)), dma((2, nx)),
        dma((3,)), dma((3,)), dma((3, ngroup)), dma((3, ngroup)), dma((4,)), dma((4,)), dma((ngroup, 4)), dma((ngroup, 4)),
        dma((2, 6, ngroup)), dma((2, 6, ngroup)), dma((2, ngroup)), dma((2, ngroup)),
        dma((ngroup,)), dma((ngroup,)), dma((4,)), dma((4,)), dma((2, 6)), dma((2, 6)),
    ]
    block = jax.ShapeDtypeStruct((tok, width), BF16)
    shapes = [block, block, block, jax.ShapeDtypeStruct((wr1, ff), BF16), jax.ShapeDtypeStruct((wr2, width), BF16)]
    hbm = pl.BlockSpec(memory_space=pl.ANY)
    small = pl.BlockSpec(memory_space=pltpu.VMEM)
    results = pl.pallas_call(
        functools.partial(kernel, nx, ny, nexp, group),
        out_shape=shapes,
        in_specs=[small] * 2 + [hbm] * 7,
        out_specs=[hbm] * 5,
        scratch_shapes=scratch,
        compiler_params=pltpu.CompilerParams(
            collective_id=0, has_side_effects=True, vmem_limit_bytes=60 * 1024 * 1024
        ),
        name="block_backward",
    )(
        expert_ids[0].T, gate_weights[0].T, queries[0], key_states[0], value_states[0], attended[0], output_grad[0],
        w_in[0], w_out[0],
    )
    results = pl.pallas_call(
        hand_out, out_shape=shapes, in_specs=[small] * 5, out_specs=[small] * 5, name="hand_out"
    )(*results)
    return tuple(r[None] for r in results)


def solution(mesh):
    stream = P("exp", "ctx", None)
    return jax.shard_map(
        per_device,
        mesh=mesh,
        in_specs=(stream,) * 7 + (P("exp", None, None),) * 2,
        out_specs=(stream,) * 5,
        check_vma=False,
    )
```

```python
import functools

import jax
import jax.numpy as jnp
from jax import lax
from jax.experimental import pallas as pl
from jax.experimental.pallas import tpu as pltpu
from jax.sharding import PartitionSpec as P

HEAD_DIM = 128
MESH = pl.DeviceIdType.MESH
F32 = jnp.float32
BF16 = jnp.bfloat16
LAG = 2
AHEAD = 2
EARLY = 1


def dot_nn(a, b):
    return lax.dot_general(a, b, (((1,), (0,)), ((), ())), preferred_element_type=F32)


def dot_nt(a, b):
    return lax.dot_general(a, b, (((1,), (1,)), ((), ())), preferred_element_type=F32)


def dot_tn(a, b):
    return lax.dot_general(a, b, (((0,), (0,)), ((), ())), preferred_element_type=F32)


def kernel(
    nx, ny, nexp, group,
    ids_ref, gates_ref, q_ref, k_ref, v_ref, att_ref, og_ref, w1_ref, w2_ref,
    qg_ref, kg_ref, vg_ref, w1g_ref, w2g_ref,
    att, og, w1, w2, code, gate_row, pick, pick_t, slot_gate, wide,
    send_rows, send_grads, send_back, got_rows, got_grads, got_back,
    rows, grads, upper, act, upg, stage, back,
    q_all, k_all, v_all, g_all, probs, sums, got_sums, inverse, delta,
    dq, dk, dv, dq_pair, dq_far, dk_far, dv_far, dk_relay, dv_relay,
    t1, t2, t1_pair, t2_pair, t1_x, t2_x, t1_relay, t2_relay, t1_z, t2_z, out1, out2,
    local_sem, out_sem, a2a_send, a2a_recv, back_send, back_recv, kv_send, kv_recv, q_send, q_recv, g_send, g_recv,
    sum_send, sum_recv, delta_send, delta_recv,
    rx_send, rx_recv, rq_send, rq_recv, rz_send, rz_recv, w_send, w_recv, wx_send, wx_recv,
):
    tok, width = att.shape
    ff = act.shape[1]
    heads = width // HEAD_DIM
    cap = send_rows.shape[1]
    scale = HEAD_DIM ** (-0.5)
    nz = nexp // ny
    gw = group * HEAD_DIM
    ngroup = heads // group
    me = lax.axis_index("exp")
    ctx = lax.axis_index("ctx")
    my_y, my_zh = lax.rem(me, ny), me // ny
    core = lax.rem(ctx, 2)
    my_x = lax.rem(ctx // 2, nx)
    zl = ctx // (2 * nx)
    b_me = zl * 2 + core

    place = ((zl, 0), (0, 1 + zl), (1 - zl, 3), (1, 1 + zl))
    origin = ((0, zl), (1 + 2 * zl, 0), (1 + 2 * zl, 1), (2, 1 - zl))

    def owner(dy, s):
        return lax.rem(my_zh + s, nz) * ny + lax.rem(my_y + dy, ny)

    def worker(dy, s):
        return {"exp": owner(dy, s), "ctx": ctx_of(place[s][0], my_x, core)}

    def source(dy, r):
        s, z = origin[r]
        return {
            "exp": lax.rem(my_zh + nz - s, nz) * ny + lax.rem(my_y + ny - dy, ny), "ctx": ctx_of(z, my_x, core)
        }

    def chunks(first, last, body):
        @pl.loop(first, last)
        def _(dy):
            for n in range(nz):
                if n == 0:
                    pl.when(dy > 0)(functools.partial(body, dy, n))
                else:
                    body(dy, n)

    def ctx_of(z, x, c):
        return (z * nx + x) * 2 + c

    def b_dev(b):
        return {"ctx": ctx_of(b // 2, my_x, lax.rem(b, 2))}

    def x_dev(x):
        return {"ctx": ctx_of(zl, x, core)}

    sib = {"ctx": ctx_of(zl, my_x, 1 - core)}
    zpart = {"ctx": ctx_of(1 - zl, my_x, core)}
    b_sib, b_z, b_diag = zl * 2 + 1 - core, (1 - zl) * 2 + core, (1 - zl) * 2 + 1 - core

    def remote(src, dst, ssem, rsem, dev):
        return pltpu.make_async_remote_copy(
            src_ref=src, dst_ref=dst, send_sem=ssem, recv_sem=rsem, device_id=dev, device_id_type=MESH
        )

    def blk(ref, i):
        return ref.at[pl.ds(pl.multiple_of(i * tok, tok), tok)]

    def cols(j, size):
        return pl.ds(pl.multiple_of(j * size, 128), size)

    def part(ref, i, g):
        return ref.at[pl.ds(pl.multiple_of(i * tok, tok), tok), cols(g, gw)]

    def slots(p):
        return pl.ds(pl.multiple_of(p * cap, 8), cap)

    barrier = pltpu.get_barrier_semaphore()

    def greet(dev):
        pl.semaphore_signal(barrier, inc=1, device_id=dev, device_id_type=MESH)

    chunks(0, ny, lambda dy, n: greet(worker(dy, n)))

    @pl.loop(0, ny)
    def _(dy):
        greet({"exp": owner(dy, 3 - 2 * zl), "ctx": ctx})

    @pl.loop(1, nx)
    def _(k):
        pl.semaphore_signal(barrier, inc=1, device_id=x_dev(lax.rem(my_x + k, nx)), device_id_type=MESH)

    @pl.loop(1, 4)
    def _(k):
        pl.semaphore_signal(barrier, inc=1, device_id=b_dev(lax.rem(b_me + k, 4)), device_id_type=MESH)

    local = [
        pltpu.make_async_copy(s, d, local_sem.at[i])
        for i, (s, d) in enumerate(
            (
                (att_ref, att), (og_ref, og), (w1_ref, w1), (w2_ref, w2),
                (q_ref, blk(q_all, b_me)), (k_ref, blk(k_all, my_x)), (v_ref, blk(v_all, my_x)),
            )
        )
    ]
    for c in local:
        c.start()

    expert = lax.broadcasted_iota(jnp.int32, (nexp, tok), 0)
    first, second = ids_ref[0:1, :] == expert, ids_ref[1:2, :] == expert
    member = jnp.where(first | second, 1.0, 0.0)
    earlier = jnp.where(
        lax.broadcasted_iota(jnp.int32, (tok, tok), 0) < lax.broadcasted_iota(jnp.int32, (tok, tok), 1), 1.0, 0.0
    )
    before = dot_nn(member.astype(BF16), earlier.astype(BF16))
    code[...] = jnp.where(member > 0.5, before, -1.0)
    gate_row[...] = jnp.where(first, gates_ref[0:1, :], 0.0) + jnp.where(second, gates_ref[1:2, :], 0.0)
    slot = lax.broadcasted_iota(jnp.int32, (cap, tok), 0).astype(F32)

    @pl.loop(0, nexp)
    def _(p):
        e = owner(p // nz, lax.rem(p, nz))
        here = jnp.broadcast_to(code[pl.ds(e, 1), :], (cap, tok)) == slot
        gate = jnp.broadcast_to(gate_row[pl.ds(e, 1), :], (cap, tok))
        wide[slots(p), pl.ds(0, tok)] = jnp.where(here, 1.0, 0.0)
        slot_gate[slots(p), :] = jnp.broadcast_to(
            jnp.sum(jnp.where(here, gate, 0.0), axis=1, keepdims=True), (cap, tok)
        )

    picked = wide[:, pl.ds(0, tok)]
    pick[...] = picked.astype(BF16)
    pick_t[...] = picked.T.astype(BF16)

    def tiles(n, size):
        return pl.loop(0, n // size)

    wide_tile = 256
    nhalf = nexp // 2
    hrows = nhalf * cap

    hy = ny // 2

    def a2a(which, dy, s):
        buffer, got = ((send_rows, got_rows), (send_grads, got_grads))[which]
        here, there = dy * nz + s, dy * nz + place[s][1]
        return remote(
            buffer.at[here], got.at[there], a2a_send.at[which, here], a2a_recv.at[which, there], worker(dy, s)
        )

    def fill(which, half):
        r = pl.ds(half * hrows, hrows)
        source, buffer = ((att, send_rows), (og, send_grads))[which]

        @tiles(width, wide_tile)
        def _(j):
            value = dot_nn(pick[r, :], source[:, cols(j, wide_tile)])
            wide[r, cols(j, wide_tile)] = value if which == 0 else value * slot_gate[r, 0:1]

        @pl.loop(half * nhalf, (half + 1) * nhalf)
        def _(p):
            buffer[p] = wide[slots(p), :].astype(BF16)

    def send(which, half):
        chunks(half * hy, (half + 1) * hy, lambda dy, s: a2a(which, dy, s).start())

    def arrived(which, half):
        buffer, got = ((send_rows, got_rows), (send_grads, got_grads))[which]

        def take(dy, r):
            p = dy * nz + r
            remote(buffer.at[p], got.at[p], a2a_send.at[which, p], a2a_recv.at[which, p], source(dy, r)).wait_recv()
            wide[slots(p), :] = got[p].astype(F32)

        if half == 0:
            wide[slots(0), :] = got[0].astype(F32)
        chunks(half * hy, (half + 1) * hy, take)

    local[0].wait()
    fill(0, 0)
    pl.semaphore_wait(barrier, nexp - 1 + ny + nx - 1 + 3)
    send(0, 0)

    q_sends = [
        remote(q_ref, blk(q_all, b_me), q_send.at[i], q_recv.at[i], dev) for i, dev in enumerate((sib, zpart))
    ]
    for c in q_sends:
        c.start()

    def kv_copy(which, k):
        src, buf = ((k_ref, k_all), (v_ref, v_all))[which]
        return remote(
            src, blk(buf, my_x), kv_send.at[which, k], kv_recv.at[which, k], x_dev(lax.rem(my_x + k, nx))
        )

    for k in range(1, nx):
        kv_copy(0, k).start()

    local[1].wait()
    fill(1, 0)
    send(1, 0)
    fill(0, 1)
    send(0, 1)
    fill(1, 1)
    send(1, 1)
    for k in range(1, nx):
        kv_copy(1, k).start()
    got_rows[0] = send_rows[0]
    got_grads[0] = send_grads[0]

    def kv_wait(which, buf):
        for k in range(1, nx):
            x = lax.rem(my_x + nx - k, nx)
            remote(blk(buf, x), blk(buf, x), kv_send.at[which, k], kv_recv.at[which, k], x_dev(x)).wait_recv()

    t = min(256, ff)
    def back_copy(g, dy, r):
        here, there = dy * nz + r, dy * nz + origin[r][0]
        return remote(
            send_back.at[g, here], got_back.at[g, there], back_send.at[g, here], back_recv.at[g, there], source(dy, r)
        )

    def back_wait(g, dy, s):
        p = dy * nz + s
        remote(
            send_back.at[g, p], got_back.at[g, p], back_send.at[g, p], back_recv.at[g, p], worker(dy, s)
        ).wait_recv()

    def expert_half(half):
        r = pl.ds(half * hrows, hrows)

        def unpack(out):
            @tiles(width, wide_tile)
            def _(j):
                out[r, cols(j, wide_tile)] = wide[r, cols(j, wide_tile)].astype(BF16)

        arrived(0, half)
        unpack(rows)
        if half == 0:
            local[2].wait()
            local[3].wait()

        @tiles(ff, t)
        def _(j):
            upper[:, cols(j, t)] = dot_nn(rows[r, :], w1[:, cols(j, t)])

        arrived(1, half)

        if half == 1:

            @pl.loop(0, EARLY)
            def _(g):
                return_group(g, 0)

        unpack(grads)

        @tiles(ff, t)
        def _(j):
            u = upper[:, cols(j, t)]
            sig = jax.nn.sigmoid(u)
            act[r, cols(j, t)] = (u * sig).astype(BF16)
            d = dot_nt(grads[r, :], w2[cols(j, t), :])
            upg[r, cols(j, t)] = (d * sig * (1.0 + u * (1.0 - sig))).astype(BF16)

    nblk = nx * 4
    wr1, wr2 = width // nblk, ff // nblk

    def half_term1(half):
        r = pl.ds(half * hrows, hrows)

        @pl.loop(0, 4)
        def _(j):
            term = dot_tn(rows[r, cols(j, width // 4)], upg[r, :])
            for i in range(nx):
                part1 = term[i * wr1 : (i + 1) * wr1]
                at = (i % 2, j * (nx // 2) + i // 2)
                t1[at] = (part1 + t1[at].astype(F32) if half else part1).astype(BF16)

    def half_term2(half):
        r = pl.ds(half * hrows, hrows)

        @pl.loop(0, 2)
        def _(j):
            term = dot_tn(act[r, cols(j, ff // 2)], grads[r, :])
            for i in range(2 * nx):
                part2 = term[i * wr2 : (i + 1) * wr2]
                at = (i % 2, j * nx + i // 2)
                t2[at] = (part2 + t2[at].astype(F32) if half else part2).astype(BF16)

    def return_group(g, half):
        chunks(half * hy, (half + 1) * hy, lambda dy, r: back_copy(g, dy, r).start())

    def row_back(half):
        r = pl.ds(half * hrows, hrows)

        @pl.loop(0, ngroup)
        def _(g):
            stage[r, :] = dot_nt(upg[r, :], w1[cols(g, gw), :])

            @pl.loop(half * nhalf, (half + 1) * nhalf)
            def _(p):
                send_back[g, p] = stage[slots(p), :].astype(BF16)

            @pl.when(g < (AHEAD if half else 0))
            def _():
                @pl.when(g >= EARLY)
                def _():
                    return_group(g, 0)

                return_group(g, half)

    expert_half(0)
    row_back(0)

    def q_forward():
        mine = blk(q_all, b_z)
        return remote(mine, mine, q_send.at[2], q_recv.at[2], sib)

    z, s, d = blk(q_all, b_z), blk(q_all, b_sib), blk(q_all, b_diag)
    remote(z, z, q_send.at[1], q_recv.at[1], zpart).wait_recv()
    q_forward().start()
    local[4].wait()
    local[5].wait()
    local[6].wait()
    kv_wait(0, k_all)
    remote(s, s, q_send.at[0], q_recv.at[0], sib).wait_recv()
    remote(d, d, q_send.at[2], q_recv.at[2], sib).wait_recv()
    sums[...] = jnp.ones_like(sums)
    nkeys, nq = nx * tok, 4 * tok
    part_keys = 2 * tok

    @pl.loop(0, heads)
    def _(h):
        c = cols(h, HEAD_DIM)
        qh = q_all[:, c]
        total = jnp.zeros((1, nq), F32)
        for i in range(nkeys // part_keys):
            e = jnp.exp(dot_nt(k_all[pl.ds(i * part_keys, part_keys), c], qh) * scale)
            probs[h, pl.ds(i * part_keys, part_keys), :] = e.astype(BF16)
            total = total + jnp.sum(e, axis=0, keepdims=True)
        sums[pl.ds(h, 1), :] = total

    def sum_copy(k):
        return remote(
            sums, got_sums.at[b_me], sum_send.at[k], sum_recv.at[k], b_dev(lax.rem(b_me + k, 4))
        )

    for k in range(1, 4):
        sum_copy(k).start()

    half_term1(0)
    half_term2(0)

    expert_half(1)

    x_next, x_far, x_prev = (lax.rem(my_x + k, nx) for k in range(1, 4))
    w_pair = (
        remote(t1.at[1 - core], t1_pair, w_send.at[0], w_recv.at[0], sib),
        remote(t2.at[1 - core], t2_pair, w_send.at[1], w_recv.at[1], sib),
    )

    half_term1(1)
    w_pair[0].start()

    row_back(1)
    half_term2(1)
    w_pair[1].start()

    def w_first(w):
        t, land, relay = ((t1, t1_x, t1_relay), (t2, t2_x, t2_relay))[w]
        return [
            remote(t.at[1 - core, i * nx + to], dst, wx_send.at[w, n], wx_recv.at[w, n], x_dev(dev))
            for n, (i, to, dst, dev) in enumerate(
                (
                    (0, x_far, relay.at[0], x_next), (1, x_far, relay.at[1], x_prev),
                    (1, x_next, land.at[0, 1], x_next), (0, x_prev, land.at[1, 0], x_prev),
                )
            )
        ]

    def w_second(w):
        t, land = ((t1, t1_x), (t2, t2_x))[w]
        return [
            remote(t.at[1 - core, i * nx + to], land.at[n, i], wx_send.at[w, 4 + n], wx_recv.at[w, 4 + n], x_dev(to))
            for n, (i, to) in enumerate(((0, x_next), (1, x_prev)))
        ]

    for w, (t, pair) in enumerate(((t1, t1_pair), (t2, t2_pair))):
        w_pair[w].wait()

        @pl.loop(0, 2 * nx)
        def _(q):
            t[1 - core, q] = (t[core, q].astype(F32) + pair[q].astype(F32)).astype(BF16)

        for c in w_first(w):
            c.start()

    def w_relay():
        for w, (t, relay) in enumerate(((t1, t1_relay), (t2, t2_relay))):
            for n, c in enumerate(w_first(w)[:2]):
                c.wait_recv()
                q = n * nx + (x_next, x_prev)[n]
                t[1 - core, q] = (t[1 - core, q].astype(F32) + relay[n].astype(F32)).astype(BF16)
                w_second(w)[n].start()

    w_z = (
        remote(t1.at[core, 1 - zl], t1_z, w_send.at[2], w_recv.at[2], zpart),
        remote(t2.at[core, 1 - zl], t2_z, w_send.at[3], w_recv.at[3], zpart),
    )

    def w_over_z():
        for w, (t, land) in enumerate(((t1, t1_x), (t2, t2_x))):
            for c in w_first(w)[2:] + w_second(w):
                c.wait_recv()
            for i in range(2):
                total = t[1 - core, i * nx + my_x].astype(F32) + land[0, i].astype(F32) + land[1, i].astype(F32)
                t[core, i] = total.astype(BF16)
            w_z[w].start()

    for k in range(1, 4):
        b = lax.rem(b_me + 4 - k, 4)
        remote(sums, got_sums.at[b], sum_send.at[k], sum_recv.at[k], b_dev(b)).wait_recv()
    got_sums[b_me] = sums[...]
    inverse[...] = 1.0 / (got_sums[0] + got_sums[1] + got_sums[2] + got_sums[3])
    kv_wait(1, v_all)

    mine = pl.ds(pl.multiple_of(b_me * tok, tok), tok)
    ones = jnp.ones((8, HEAD_DIM), F32)

    def g_sends(g):
        m = part(g_all, b_me, g)
        return [remote(m, m, g_send.at[i, g], g_recv.at[i, g], dev) for i, dev in enumerate((sib, zpart))]

    def g_forward(g):
        m = part(g_all, b_z, g)
        return remote(m, m, g_send.at[2, g], g_recv.at[2, g], sib)

    def delta_copy(g, k):
        m = delta.at[g, b_me]
        return remote(m, m, delta_send.at[g, k], delta_recv.at[g, k], b_dev(lax.rem(b_me + k, 4)))

    def combine(g):
        def take(dy, n):
            back_wait(g, dy, n)
            p = dy * nz + n
            stage[slots(p), :] = got_back[g, p].astype(F32)

        stage[slots(0), :] = send_back[g, 0].astype(F32)
        chunks(0, ny, take)
        back[...] = stage[...].astype(BF16)
        c = cols(g, gw)
        total = (og[:, c].astype(F32) + dot_nn(pick_t[...], back[...])).astype(BF16)
        g_all[mine, c] = total
        for d in g_sends(g):
            d.start()

        @pl.when(g + AHEAD < ngroup)
        def _():
            @pl.when(g + AHEAD >= EARLY)
            def _():
                return_group(g + AHEAD, 0)

            return_group(g + AHEAD, 1)

        prod = total.astype(F32) * att[:, c].astype(F32)
        for i in range(group):
            d = lax.dot_general(
                ones, prod[:, i * HEAD_DIM : (i + 1) * HEAD_DIM], (((1,), (1,)), ((), ())),
                preferred_element_type=F32, precision=lax.Precision.HIGHEST,
            )
            delta[g, b_me, i : i + 1, :] = d[0:1, :]
        for k in range(1, 4):
            delta_copy(g, k).start()

    def forward(g):
        m = part(g_all, b_z, g)
        remote(m, m, g_send.at[1, g], g_recv.at[1, g], zpart).wait_recv()
        g_forward(g).start()

    def gathered(g):
        for k in range(1, 4):
            b = lax.rem(b_me + 4 - k, 4)
            m = delta.at[g, b]
            remote(m, m, delta_send.at[g, k], delta_recv.at[g, k], b_dev(b)).wait_recv()
        m = part(g_all, b_sib, g)
        remote(m, m, g_send.at[0, g], g_recv.at[0, g], sib).wait_recv()
        m = part(g_all, b_diag, g)
        remote(m, m, g_send.at[2, g], g_recv.at[2, g], sib).wait_recv()

    half_block = tok // 2

    def half_part(ref, i, n, g):
        return ref.at[pl.ds(pl.multiple_of(i * tok + n * half_block, half_block), half_block), cols(g, gw)]

    def half_of(ref, k, n, g):
        return ref.at[k, pl.ds(n * half_block, half_block), cols(g, gw)]

    kv_parts = ((dk, dk_far, dk_relay), (dv, dv_far, dv_relay))

    def x_first(w, g):
        src, far, relay = kv_parts[w]
        return [
            remote(half_part(src, to, i, g), dst, rx_send.at[w, n, g], rx_recv.at[w, n, g], x_dev(dev))
            for n, (i, to, dst, dev) in enumerate(
                (
                    (0, x_far, relay.at[0, :, cols(g, gw)], x_next), (1, x_far, relay.at[1, :, cols(g, gw)], x_prev),
                    (1, x_next, half_of(far, 0, 1, g), x_next), (0, x_prev, half_of(far, 1, 0, g), x_prev),
                )
            )
        ]

    def x_second(w, g):
        src, far, _ = kv_parts[w]
        return [
            remote(
                half_part(src, to, n, g), half_of(far, n, n, g), rx_send.at[w, 4 + n, g], rx_recv.at[w, 4 + n, g], x_dev(to)
            )
            for n, to in enumerate((x_next, x_prev))
        ]

    def x_relay(g):
        for w, (src, _, relay) in enumerate(kv_parts):
            for n, c in enumerate(x_first(w, g)[:2]):
                c.wait_recv()
                r = pl.ds(pl.multiple_of((x_next, x_prev)[n] * tok + n * half_block, half_block), half_block)
                k = cols(g, gw)
                src[r, k] = (src[r, k].astype(F32) + relay[n, :, k].astype(F32)).astype(BF16)
                x_second(w, g)[n].start()

    def pair_copies(g):
        return [
            remote(
                part(dq, i * 2 + 1 - core, g), dq_pair.at[i, :, cols(g, gw)], rq_send.at[i, g], rq_recv.at[i, g], sib
            )
            for i in range(2)
        ]

    def far_copy(g):
        return remote(part(dq, b_z, g), dq_far.at[:, cols(g, gw)], rz_send.at[g], rz_recv.at[g], zpart)

    def attention(g):
        gathered(g)

        @pl.loop(0, group)
        def _(i):
            h = g * group + i
            c = cols(h, HEAD_DIM)
            qh, gh = q_all[:, c], g_all[:, c]
            inv = inverse[pl.ds(h, 1), :]
            dl = jnp.concatenate([delta[g, b, pl.ds(i, 1), :] for b in range(4)], axis=1)
            q_acc = jnp.zeros((nq, HEAD_DIM), F32)
            for n in range(nkeys // part_keys):
                r = pl.ds(n * part_keys, part_keys)
                kh = k_all[r, c]
                p = probs[h, r, :].astype(F32) * inv
                s = (p * (dot_nt(v_all[r, c], gh) - dl)).astype(BF16)
                dv[r, c] = dot_nn(p.astype(BF16), gh).astype(BF16)
                dk[r, c] = (dot_nn(s, qh) * scale).astype(BF16)
                q_acc = q_acc + dot_tn(s, kh)
            dq[:, c] = (q_acc * scale).astype(BF16)

        for w in range(2):
            for c in x_first(w, g):
                c.start()
        for c in pair_copies(g):
            c.start()

    def second_step(g):
        for c in pair_copies(g):
            c.wait_recv()
        rows_z = pl.ds(pl.multiple_of(b_z * tok, tok), tok)
        dq[rows_z, cols(g, gw)] = (
            dq[rows_z, cols(g, gw)].astype(F32) + dq_pair[1 - zl, :, cols(g, gw)].astype(F32)
        ).astype(BF16)
        far_copy(g).start()

    def first_sent():
        def sent(dy, n):
            a2a(0, dy, n).wait_send()
            a2a(1, dy, n).wait_send()

        chunks(0, ny, sent)
        for c in q_sends:
            c.wait_send()
        q_forward().wait_send()
        for which in range(2):
            for k in range(1, nx):
                kv_copy(which, k).wait_send()
        for k in range(1, 4):
            sum_copy(k).wait_send()

    def back_sent(g):
        chunks(0, ny, lambda dy, n: back_copy(g, dy, n).wait_send())

    def group_sent(g):
        for c in g_sends(g):
            c.wait_send()
        g_forward(g).wait_send()
        for k in range(1, 4):
            delta_copy(g, k).wait_send()
        for c in pair_copies(g):
            c.wait_send()
        for w in range(2):
            for c in x_first(w, g) + x_second(w, g):
                c.wait_send()
        far_copy(g).wait_send()

    @pl.loop(0, ngroup + LAG)
    def _(step):
        @pl.when((step >= 1) & (step <= ngroup))
        def _():
            forward(step - 1)

        @pl.when(step < ngroup)
        def _():
            combine(step)

        @pl.when((step >= 1) & (step <= ngroup))
        def _():
            attention(step - 1)

        @pl.when((step >= 2) & (step < ngroup + 2))
        def _():
            second_step(step - 2)

        @pl.when(step == 1)
        def _():
            w_relay()

        @pl.when(step >= LAG)
        def _():
            x_relay(step - LAG)

        @pl.when(step == 2)
        def _():
            first_sent()

        @pl.when(step == ngroup)
        def _():
            w_over_z()

            @pl.loop(0, ngroup)
            def _(g):
                back_sent(g)

            for w in range(2):
                for c in w_first(w) + w_second(w):
                    c.wait_send()

    rows_x = pl.ds(pl.multiple_of(my_x * tok, tok), tok)

    @pl.loop(0, ngroup)
    def _(g):
        c = cols(g, gw)

        @pl.when(g > 0)
        def _():
            group_sent(g - 1)

        far_copy(g).wait_recv()
        dq[mine, c] = (
            dq[mine, c].astype(F32) + dq_pair[zl, :, c].astype(F32) + dq_far[:, c].astype(F32)
        ).astype(BF16)
        for w, (src, far, _) in enumerate(kv_parts):
            for d in x_first(w, g)[2:] + x_second(w, g):
                d.wait_recv()
            src[rows_x, c] = (
                src[rows_x, c].astype(F32) + far[0, :, c].astype(F32) + far[1, :, c].astype(F32)
            ).astype(BF16)

    outs = [
        pltpu.make_async_copy(blk(dq, b_me), qg_ref, out_sem.at[0]),
        pltpu.make_async_copy(blk(dk, my_x), kg_ref, out_sem.at[1]),
        pltpu.make_async_copy(blk(dv, my_x), vg_ref, out_sem.at[2]),
    ]
    for c in outs:
        c.start()
    for c in w_z:
        c.wait()
    out1[...] = (t1[core, zl].astype(F32) + t1_z[...].astype(F32)).astype(BF16)
    out2[...] = (t2[core, zl].astype(F32) + t2_z[...].astype(F32)).astype(BF16)
    outs += [
        pltpu.make_async_copy(out1, w1g_ref, out_sem.at[3]),
        pltpu.make_async_copy(out2, w2g_ref, out_sem.at[4]),
    ]
    for c in outs[3:]:
        c.start()

    for g in range(ngroup - 1, ngroup):
        group_sent(g)

    for c in outs:
        c.wait()


def hand_out(*refs):
    n = len(refs) // 2
    for i in range(n):
        refs[n + i][...] = refs[i][...]


def per_device(queries, key_states, value_states, attended, output_grad, expert_ids, gate_weights, w_in, w_out):
    tok, width = queries.shape[1:]
    ff = w_in.shape[2]
    heads = width // HEAD_DIM
    nexp, nctx = lax.axis_size("exp"), lax.axis_size("ctx")
    nx, ny = nctx // 4, nexp // 4
    cap = 3 * tok // nexp
    pairs = nexp * cap
    group = 3 if heads % 3 == 0 else 2
    ngroup, gw = heads // group, group * HEAD_DIM
    hp = -(-heads // 8) * 8
    wr1, wr2 = width // nctx, ff // nctx
    dma = pltpu.SemaphoreType.DMA
    v = pltpu.VMEM
    scratch = [
        v((tok, width), BF16), v((tok, width), BF16), v((width, ff), BF16), v((ff, width), BF16),
        v((nexp, tok), F32), v((nexp, tok), F32), v((pairs, tok), BF16), v((tok, pairs), BF16),
        v((pairs, tok), F32), v((pairs, width), F32),
        v((nexp, cap, width), BF16), v((nexp, cap, width), BF16), v((ngroup, nexp, cap, gw), BF16),
        v((nexp, cap, width), BF16), v((nexp, cap, width), BF16), v((ngroup, nexp, cap, gw), BF16),
        v((pairs, width), BF16), v((pairs, width), BF16), v((pairs // 2, ff), F32), v((pairs, ff), BF16), v((pairs, ff), BF16),
        v((pairs, gw), F32), v((pairs, gw), BF16),
        v((4 * tok, width), BF16), v((nx * tok, width), BF16), v((nx * tok, width), BF16), v((4 * tok, width), BF16),
        v((heads, nx * tok, 4 * tok), BF16),
        v((hp, 4 * tok), F32), v((4, hp, 4 * tok), F32), v((hp, 4 * tok), F32), v((ngroup, 4, 8, tok), F32),
        v((4 * tok, width), BF16), v((nx * tok, width), BF16), v((nx * tok, width), BF16),
        v((2, tok, width), BF16), v((tok, width), BF16),
        v((2, tok, width), BF16), v((2, tok, width), BF16),
        v((2, tok // 2, width), BF16), v((2, tok // 2, width), BF16),
        v((2, 2 * nx, wr1, ff), BF16), v((2, 2 * nx, wr2, width), BF16),
        v((2 * nx, wr1, ff), BF16), v((2 * nx, wr2, width), BF16),
        v((2, 2, wr1, ff), BF16), v((2, 2, wr2, width), BF16), v((2, wr1, ff), BF16), v((2, wr2, width), BF16),
        v((wr1, ff), BF16), v((wr2, width), BF16), v((wr1, ff), BF16), v((wr2, width), BF16),
        dma((7,)), dma((5,)), dma((2, nexp)), dma((2, nexp)), dma((ngroup, nexp)), dma((ngroup, nexp)), dma((2, nx)), dma((2, nx)),
        dma((3,)), dma((3,)), dma((3, ngroup)), dma((3, ngroup)), dma((4,)), dma((4,)), dma((ngroup, 4)), dma((ngroup, 4)),
        dma((2, 6, ngroup)), dma((2, 6, ngroup)), dma((2, ngroup)), dma((2, ngroup)),
        dma((ngroup,)), dma((ngroup,)), dma((4,)), dma((4,)), dma((2, 6)), dma((2, 6)),
    ]
    block = jax.ShapeDtypeStruct((tok, width), BF16)
    shapes = [block, block, block, jax.ShapeDtypeStruct((wr1, ff), BF16), jax.ShapeDtypeStruct((wr2, width), BF16)]
    hbm = pl.BlockSpec(memory_space=pl.ANY)
    small = pl.BlockSpec(memory_space=pltpu.VMEM)
    results = pl.pallas_call(
        functools.partial(kernel, nx, ny, nexp, group),
        out_shape=shapes,
        in_specs=[small] * 2 + [hbm] * 7,
        out_specs=[hbm] * 5,
        scratch_shapes=scratch,
        compiler_params=pltpu.CompilerParams(
            collective_id=0, has_side_effects=True, vmem_limit_bytes=60 * 1024 * 1024
        ),
        name="block_backward",
    )(
        expert_ids[0].T, gate_weights[0].T, queries[0], key_states[0], value_states[0], attended[0], output_grad[0],
        w_in[0], w_out[0],
    )
    results = pl.pallas_call(
        hand_out, out_shape=shapes, in_specs=[small] * 5, out_specs=[small] * 5, name="hand_out"
    )(*results)
    return tuple(r[None] for r in results)


def solution(mesh):
    stream = P("exp", "ctx", None)
    return jax.shard_map(
        per_device,
        mesh=mesh,
        in_specs=(stream,) * 7 + (P("exp", None, None),) * 2,
        out_specs=(stream,) * 5,
        check_vma=False,
    )
```

```python
import functools

import jax
import jax.numpy as jnp
from jax import lax
from jax.experimental import pallas as pl
from jax.experimental.pallas import tpu as pltpu
from jax.sharding import PartitionSpec as P

HEAD_DIM = 128
MESH = pl.DeviceIdType.MESH
F32 = jnp.float32
BF16 = jnp.bfloat16
LAG = 2
AHEAD = 2
EARLY = 1


def dot_nn(a, b):
    return lax.dot_general(a, b, (((1,), (0,)), ((), ())), preferred_element_type=F32)


def dot_nt(a, b):
    return lax.dot_general(a, b, (((1,), (1,)), ((), ())), preferred_element_type=F32)


def dot_tn(a, b):
    return lax.dot_general(a, b, (((0,), (0,)), ((), ())), preferred_element_type=F32)


def kernel(
    nx, ny, nexp, group,
    ids_ref, gates_ref, q_ref, k_ref, v_ref, att_ref, og_ref, w1_ref, w2_ref,
    qg_ref, kg_ref, vg_ref, w1g_ref, w2g_ref,
    att, og, w1, w2, code, gate_row, pick, pick_t, slot_gate, wide,
    send_rows, send_grads, send_back, got_rows, got_grads, got_back,
    rows, grads, upper, act, upg, stage, back,
    q_all, k_all, v_all, g_all, probs, sums, got_sums, inverse, delta,
    dq, dk, dv, dq_pair, dq_far, dk_far, dv_far, dk_relay, dv_relay,
    t1, t2, t1_pair, t2_pair, t1_x, t2_x, t1_relay, t2_relay, t1_z, t2_z, out1, out2,
    local_sem, out_sem, a2a_send, a2a_recv, back_send, back_recv, kv_send, kv_recv, q_send, q_recv, g_send, g_recv,
    sum_send, sum_recv, delta_send, delta_recv,
    rx_send, rx_recv, rq_send, rq_recv, rz_send, rz_recv, w_send, w_recv, wx_send, wx_recv,
):
    tok, width = att.shape
    ff = act.shape[1]
    heads = width // HEAD_DIM
    cap = send_rows.shape[1]
    scale = HEAD_DIM ** (-0.5)
    nz = nexp // ny
    gw = group * HEAD_DIM
    ngroup = heads // group
    me = lax.axis_index("exp")
    ctx = lax.axis_index("ctx")
    my_y, my_zh = lax.rem(me, ny), me // ny
    core = lax.rem(ctx, 2)
    my_x = lax.rem(ctx // 2, nx)
    zl = ctx // (2 * nx)
    b_me = zl * 2 + core

    place = ((zl, 0), (0, 1 + zl), (1 - zl, 3), (1, 1 + zl))
    origin = ((0, zl), (1 + 2 * zl, 0), (1 + 2 * zl, 1), (2, 1 - zl))

    def owner(dy, s):
        return lax.rem(my_zh + s, nz) * ny + lax.rem(my_y + dy, ny)

    def worker(dy, s):
        return {"exp": owner(dy, s), "ctx": ctx_of(place[s][0], my_x, core)}

    def source(dy, r):
        s, z = origin[r]
        return {
            "exp": lax.rem(my_zh + nz - s, nz) * ny + lax.rem(my_y + ny - dy, ny), "ctx": ctx_of(z, my_x, core)
        }

    def chunks(first, last, body):
        @pl.loop(first, last)
        def _(dy):
            for n in range(nz):
                if n == 0:
                    pl.when(dy > 0)(functools.partial(body, dy, n))
                else:
                    body(dy, n)

    def ctx_of(z, x, c):
        return (z * nx + x) * 2 + c

    def b_dev(b):
        return {"ctx": ctx_of(b // 2, my_x, lax.rem(b, 2))}

    def x_dev(x):
        return {"ctx": ctx_of(zl, x, core)}

    sib = {"ctx": ctx_of(zl, my_x, 1 - core)}
    zpart = {"ctx": ctx_of(1 - zl, my_x, core)}
    b_sib, b_z, b_diag = zl * 2 + 1 - core, (1 - zl) * 2 + core, (1 - zl) * 2 + 1 - core

    def remote(src, dst, ssem, rsem, dev):
        return pltpu.make_async_remote_copy(
            src_ref=src, dst_ref=dst, send_sem=ssem, recv_sem=rsem, device_id=dev, device_id_type=MESH
        )

    def blk(ref, i):
        return ref.at[pl.ds(pl.multiple_of(i * tok, tok), tok)]

    def cols(j, size):
        return pl.ds(pl.multiple_of(j * size, 128), size)

    def part(ref, i, g):
        return ref.at[pl.ds(pl.multiple_of(i * tok, tok), tok), cols(g, gw)]

    def slots(p):
        return pl.ds(pl.multiple_of(p * cap, 8), cap)

    barrier = pltpu.get_barrier_semaphore()

    def greet(dev):
        pl.semaphore_signal(barrier, inc=1, device_id=dev, device_id_type=MESH)

    chunks(0, ny, lambda dy, n: greet(worker(dy, n)))

    @pl.loop(0, ny)
    def _(dy):
        greet({"exp": owner(dy, 3 - 2 * zl), "ctx": ctx})

    @pl.loop(1, nx)
    def _(k):
        pl.semaphore_signal(barrier, inc=1, device_id=x_dev(lax.rem(my_x + k, nx)), device_id_type=MESH)

    @pl.loop(1, 4)
    def _(k):
        pl.semaphore_signal(barrier, inc=1, device_id=b_dev(lax.rem(b_me + k, 4)), device_id_type=MESH)

    local = [
        pltpu.make_async_copy(s, d, local_sem.at[i])
        for i, (s, d) in enumerate(
            (
                (att_ref, att), (og_ref, og), (w1_ref, w1), (w2_ref, w2),
                (q_ref, blk(q_all, b_me)), (k_ref, blk(k_all, my_x)), (v_ref, blk(v_all, my_x)),
            )
        )
    ]
    for c in local:
        c.start()

    expert = lax.broadcasted_iota(jnp.int32, (nexp, tok), 0)
    first, second = ids_ref[0:1, :] == expert, ids_ref[1:2, :] == expert
    member = jnp.where(first | second, 1.0, 0.0)
    earlier = jnp.where(
        lax.broadcasted_iota(jnp.int32, (tok, tok), 0) < lax.broadcasted_iota(jnp.int32, (tok, tok), 1), 1.0, 0.0
    )
    before = dot_nn(member.astype(BF16), earlier.astype(BF16))
    code[...] = jnp.where(member > 0.5, before, -1.0)
    gate_row[...] = jnp.where(first, gates_ref[0:1, :], 0.0) + jnp.where(second, gates_ref[1:2, :], 0.0)
    slot = lax.broadcasted_iota(jnp.int32, (cap, tok), 0).astype(F32)

    @pl.loop(0, nexp)
    def _(p):
        e = owner(p // nz, lax.rem(p, nz))
        here = jnp.broadcast_to(code[pl.ds(e, 1), :], (cap, tok)) == slot
        gate = jnp.broadcast_to(gate_row[pl.ds(e, 1), :], (cap, tok))
        wide[slots(p), pl.ds(0, tok)] = jnp.where(here, 1.0, 0.0)
        slot_gate[slots(p), :] = jnp.broadcast_to(
            jnp.sum(jnp.where(here, gate, 0.0), axis=1, keepdims=True), (cap, tok)
        )

    picked = wide[:, pl.ds(0, tok)]
    pick[...] = picked.astype(BF16)
    pick_t[...] = picked.T.astype(BF16)

    def tiles(n, size):
        return pl.loop(0, n // size)

    wide_tile = 256
    nhalf = nexp // 2
    hrows = nhalf * cap

    hy = ny // 2

    def a2a(which, dy, s):
        buffer, got = ((send_rows, got_rows), (send_grads, got_grads))[which]
        here, there = dy * nz + s, dy * nz + place[s][1]
        return remote(
            buffer.at[here], got.at[there], a2a_send.at[which, here], a2a_recv.at[which, there], worker(dy, s)
        )

    def fill(which, half):
        r = pl.ds(half * hrows, hrows)
        source, buffer = ((att, send_rows), (og, send_grads))[which]

        @tiles(width, wide_tile)
        def _(j):
            value = dot_nn(pick[r, :], source[:, cols(j, wide_tile)])
            wide[r, cols(j, wide_tile)] = value if which == 0 else value * slot_gate[r, 0:1]

        @pl.loop(half * nhalf, (half + 1) * nhalf)
        def _(p):
            buffer[p] = wide[slots(p), :].astype(BF16)

    def send(which, half):
        chunks(half * hy, (half + 1) * hy, lambda dy, s: a2a(which, dy, s).start())

    def arrived(which, half):
        buffer, got = ((send_rows, got_rows), (send_grads, got_grads))[which]

        def take(dy, r):
            p = dy * nz + r
            remote(buffer.at[p], got.at[p], a2a_send.at[which, p], a2a_recv.at[which, p], source(dy, r)).wait_recv()
            wide[slots(p), :] = got[p].astype(F32)

        if half == 0:
            wide[slots(0), :] = got[0].astype(F32)
        chunks(half * hy, (half + 1) * hy, take)

    local[0].wait()
    fill(0, 0)
    pl.semaphore_wait(barrier, nexp - 1 + ny + nx - 1 + 3)
    send(0, 0)

    q_sends = [
        remote(q_ref, blk(q_all, b_me), q_send.at[i], q_recv.at[i], dev) for i, dev in enumerate((sib, zpart))
    ]
    for c in q_sends:
        c.start()

    def kv_copy(which, k):
        src, buf = ((k_ref, k_all), (v_ref, v_all))[which]
        return remote(
            src, blk(buf, my_x), kv_send.at[which, k], kv_recv.at[which, k], x_dev(lax.rem(my_x + k, nx))
        )

    for k in range(1, nx):
        kv_copy(0, k).start()

    local[1].wait()
    fill(1, 0)
    send(1, 0)
    fill(0, 1)
    send(0, 1)
    fill(1, 1)
    send(1, 1)
    for k in range(1, nx):
        kv_copy(1, k).start()
    got_rows[0] = send_rows[0]
    got_grads[0] = send_grads[0]

    def kv_wait(which, buf):
        for k in range(1, nx):
            x = lax.rem(my_x + nx - k, nx)
            remote(blk(buf, x), blk(buf, x), kv_send.at[which, k], kv_recv.at[which, k], x_dev(x)).wait_recv()

    t = min(256, ff)
    def back_copy(g, dy, r):
        here, there = dy * nz + r, dy * nz + origin[r][0]
        return remote(
            send_back.at[g, here], got_back.at[g, there], back_send.at[g, here], back_recv.at[g, there], source(dy, r)
        )

    def back_wait(g, dy, s):
        p = dy * nz + s
        remote(
            send_back.at[g, p], got_back.at[g, p], back_send.at[g, p], back_recv.at[g, p], worker(dy, s)
        ).wait_recv()

    def expert_half(half):
        r = pl.ds(half * hrows, hrows)

        def unpack(out):
            @tiles(width, wide_tile)
            def _(j):
                out[r, cols(j, wide_tile)] = wide[r, cols(j, wide_tile)].astype(BF16)

        arrived(0, half)
        unpack(rows)
        if half == 0:
            local[2].wait()
            local[3].wait()

        @tiles(ff, t)
        def _(j):
            upper[:, cols(j, t)] = dot_nn(rows[r, :], w1[:, cols(j, t)])

        arrived(1, half)

        if half == 1:

            @pl.loop(0, EARLY)
            def _(g):
                return_group(g, 0)

        unpack(grads)

        @tiles(ff, t)
        def _(j):
            u = upper[:, cols(j, t)]
            sig = jax.nn.sigmoid(u)
            act[r, cols(j, t)] = (u * sig).astype(BF16)
            d = dot_nt(grads[r, :], w2[cols(j, t), :])
            upg[r, cols(j, t)] = (d * sig * (1.0 + u * (1.0 - sig))).astype(BF16)

    nblk = nx * 4
    wr1, wr2 = width // nblk, ff // nblk

    def half_term1(half):
        r = pl.ds(half * hrows, hrows)

        @pl.loop(0, 4)
        def _(j):
            term = dot_tn(rows[r, cols(j, width // 4)], upg[r, :])
            for i in range(nx):
                part1 = term[i * wr1 : (i + 1) * wr1]
                at = (i % 2, j * (nx // 2) + i // 2)
                t1[at] = (part1 + t1[at].astype(F32) if half else part1).astype(BF16)

    def half_term2(half):
        r = pl.ds(half * hrows, hrows)

        @pl.loop(0, 2)
        def _(j):
            term = dot_tn(act[r, cols(j, ff // 2)], grads[r, :])
            for i in range(2 * nx):
                part2 = term[i * wr2 : (i + 1) * wr2]
                at = (i % 2, j * nx + i // 2)
                t2[at] = (part2 + t2[at].astype(F32) if half else part2).astype(BF16)

    def return_group(g, half):
        chunks(half * hy, (half + 1) * hy, lambda dy, r: back_copy(g, dy, r).start())

    def row_back(half):
        r = pl.ds(half * hrows, hrows)

        @pl.loop(0, ngroup)
        def _(g):
            stage[r, :] = dot_nt(upg[r, :], w1[cols(g, gw), :])

            @pl.loop(half * nhalf, (half + 1) * nhalf)
            def _(p):
                send_back[g, p] = stage[slots(p), :].astype(BF16)

            @pl.when(g < (AHEAD if half else 0))
            def _():
                @pl.when(g >= EARLY)
                def _():
                    return_group(g, 0)

                return_group(g, half)

    expert_half(0)
    row_back(0)

    def q_forward():
        mine = blk(q_all, b_z)
        return remote(mine, mine, q_send.at[2], q_recv.at[2], sib)

    z, s, d = blk(q_all, b_z), blk(q_all, b_sib), blk(q_all, b_diag)
    remote(z, z, q_send.at[1], q_recv.at[1], zpart).wait_recv()
    q_forward().start()
    local[4].wait()
    local[5].wait()
    local[6].wait()
    kv_wait(0, k_all)
    remote(s, s, q_send.at[0], q_recv.at[0], sib).wait_recv()
    remote(d, d, q_send.at[2], q_recv.at[2], sib).wait_recv()
    sums[...] = jnp.ones_like(sums)
    nkeys, nq = nx * tok, 4 * tok
    part_keys = 2 * tok

    @pl.loop(0, heads)
    def _(h):
        c = cols(h, HEAD_DIM)
        qh = q_all[:, c]
        total = jnp.zeros((1, nq), F32)
        for i in range(nkeys // part_keys):
            e = jnp.exp(dot_nt(k_all[pl.ds(i * part_keys, part_keys), c], qh) * scale)
            probs[h, pl.ds(i * part_keys, part_keys), :] = e.astype(BF16)
            total = total + jnp.sum(e, axis=0, keepdims=True)
        sums[pl.ds(h, 1), :] = total

    def sum_copy(k):
        return remote(
            sums, got_sums.at[b_me], sum_send.at[k], sum_recv.at[k], b_dev(lax.rem(b_me + k, 4))
        )

    for k in range(1, 4):
        sum_copy(k).start()

    half_term1(0)
    half_term2(0)

    expert_half(1)

    x_next, x_far, x_prev = (lax.rem(my_x + k, nx) for k in range(1, 4))
    w_pair = (
        remote(t1.at[1 - core], t1_pair, w_send.at[0], w_recv.at[0], sib),
        remote(t2.at[1 - core], t2_pair, w_send.at[1], w_recv.at[1], sib),
    )

    half_term1(1)
    w_pair[0].start()

    row_back(1)
    def w_first(w):
        t, land, relay = ((t1, t1_x, t1_relay), (t2, t2_x, t2_relay))[w]
        return [
            remote(t.at[1 - core, i * nx + to], dst, wx_send.at[w, n], wx_recv.at[w, n], x_dev(dev))
            for n, (i, to, dst, dev) in enumerate(
                (
                    (0, x_far, relay.at[0], x_next), (1, x_far, relay.at[1], x_prev),
                    (1, x_next, land.at[0, 1], x_next), (0, x_prev, land.at[1, 0], x_prev),
                )
            )
        ]

    def w_second(w):
        t, land = ((t1, t1_x), (t2, t2_x))[w]
        return [
            remote(t.at[1 - core, i * nx + to], land.at[n, i], wx_send.at[w, 4 + n], wx_recv.at[w, 4 + n], x_dev(to))
            for n, (i, to) in enumerate(((0, x_next), (1, x_prev)))
        ]

    for w, (t, pair) in enumerate(((t1, t1_pair), (t2, t2_pair))):
        if w == 1:
            half_term2(1)
            w_pair[1].start()
        w_pair[w].wait()

        @pl.loop(0, 2 * nx)
        def _(q):
            t[1 - core, q] = (t[core, q].astype(F32) + pair[q].astype(F32)).astype(BF16)

        for c in w_first(w):
            c.start()

    def w_relay():
        for w, (t, relay) in enumerate(((t1, t1_relay), (t2, t2_relay))):
            for n, c in enumerate(w_first(w)[:2]):
                c.wait_recv()
                q = n * nx + (x_next, x_prev)[n]
                t[1 - core, q] = (t[1 - core, q].astype(F32) + relay[n].astype(F32)).astype(BF16)
                w_second(w)[n].start()

    w_z = (
        remote(t1.at[core, 1 - zl], t1_z, w_send.at[2], w_recv.at[2], zpart),
        remote(t2.at[core, 1 - zl], t2_z, w_send.at[3], w_recv.at[3], zpart),
    )

    def w_over_z():
        for w, (t, land) in enumerate(((t1, t1_x), (t2, t2_x))):
            for c in w_first(w)[2:] + w_second(w):
                c.wait_recv()
            for i in range(2):
                total = t[1 - core, i * nx + my_x].astype(F32) + land[0, i].astype(F32) + land[1, i].astype(F32)
                t[core, i] = total.astype(BF16)
            w_z[w].start()

    for k in range(1, 4):
        b = lax.rem(b_me + 4 - k, 4)
        remote(sums, got_sums.at[b], sum_send.at[k], sum_recv.at[k], b_dev(b)).wait_recv()
    got_sums[b_me] = sums[...]
    inverse[...] = 1.0 / (got_sums[0] + got_sums[1] + got_sums[2] + got_sums[3])
    kv_wait(1, v_all)

    mine = pl.ds(pl.multiple_of(b_me * tok, tok), tok)
    ones = jnp.ones((8, HEAD_DIM), F32)

    def g_sends(g):
        m = part(g_all, b_me, g)
        return [remote(m, m, g_send.at[i, g], g_recv.at[i, g], dev) for i, dev in enumerate((sib, zpart))]

    def g_forward(g):
        m = part(g_all, b_z, g)
        return remote(m, m, g_send.at[2, g], g_recv.at[2, g], sib)

    def delta_copy(g, k):
        m = delta.at[g, b_me]
        return remote(m, m, delta_send.at[g, k], delta_recv.at[g, k], b_dev(lax.rem(b_me + k, 4)))

    def combine(g):
        def take(dy, n):
            back_wait(g, dy, n)
            p = dy * nz + n
            stage[slots(p), :] = got_back[g, p].astype(F32)

        stage[slots(0), :] = send_back[g, 0].astype(F32)
        chunks(0, ny, take)
        back[...] = stage[...].astype(BF16)
        c = cols(g, gw)
        total = (og[:, c].astype(F32) + dot_nn(pick_t[...], back[...])).astype(BF16)
        g_all[mine, c] = total
        for d in g_sends(g)[::-1]:
            d.start()

        @pl.when(g + AHEAD < ngroup)
        def _():
            @pl.when(g + AHEAD >= EARLY)
            def _():
                return_group(g + AHEAD, 0)

            return_group(g + AHEAD, 1)

        prod = total.astype(F32) * att[:, c].astype(F32)
        for i in range(group):
            d = lax.dot_general(
                ones, prod[:, i * HEAD_DIM : (i + 1) * HEAD_DIM], (((1,), (1,)), ((), ())),
                preferred_element_type=F32, precision=lax.Precision.HIGHEST,
            )
            delta[g, b_me, i : i + 1, :] = d[0:1, :]
        for k in range(1, 4):
            delta_copy(g, k).start()

    def forward(g):
        m = part(g_all, b_z, g)
        remote(m, m, g_send.at[1, g], g_recv.at[1, g], zpart).wait_recv()
        g_forward(g).start()

    def gathered(g):
        for k in range(1, 4):
            b = lax.rem(b_me + 4 - k, 4)
            m = delta.at[g, b]
            remote(m, m, delta_send.at[g, k], delta_recv.at[g, k], b_dev(b)).wait_recv()
        m = part(g_all, b_sib, g)
        remote(m, m, g_send.at[0, g], g_recv.at[0, g], sib).wait_recv()
        m = part(g_all, b_diag, g)
        remote(m, m, g_send.at[2, g], g_recv.at[2, g], sib).wait_recv()

    half_block = tok // 2

    def half_part(ref, i, n, g):
        return ref.at[pl.ds(pl.multiple_of(i * tok + n * half_block, half_block), half_block), cols(g, gw)]

    def half_of(ref, k, n, g):
        return ref.at[k, pl.ds(n * half_block, half_block), cols(g, gw)]

    kv_parts = ((dk, dk_far, dk_relay), (dv, dv_far, dv_relay))

    def x_first(w, g):
        src, far, relay = kv_parts[w]
        return [
            remote(half_part(src, to, i, g), dst, rx_send.at[w, n, g], rx_recv.at[w, n, g], x_dev(dev))
            for n, (i, to, dst, dev) in enumerate(
                (
                    (0, x_far, relay.at[0, :, cols(g, gw)], x_next), (1, x_far, relay.at[1, :, cols(g, gw)], x_prev),
                    (1, x_next, half_of(far, 0, 1, g), x_next), (0, x_prev, half_of(far, 1, 0, g), x_prev),
                )
            )
        ]

    def x_second(w, g):
        src, far, _ = kv_parts[w]
        return [
            remote(
                half_part(src, to, n, g), half_of(far, n, n, g), rx_send.at[w, 4 + n, g], rx_recv.at[w, 4 + n, g], x_dev(to)
            )
            for n, to in enumerate((x_next, x_prev))
        ]

    def x_relay(g):
        for w, (src, _, relay) in enumerate(kv_parts):
            for n, c in enumerate(x_first(w, g)[:2]):
                c.wait_recv()
                r = pl.ds(pl.multiple_of((x_next, x_prev)[n] * tok + n * half_block, half_block), half_block)
                k = cols(g, gw)
                src[r, k] = (src[r, k].astype(F32) + relay[n, :, k].astype(F32)).astype(BF16)
                x_second(w, g)[n].start()

    def pair_copies(g):
        return [
            remote(
                part(dq, i * 2 + 1 - core, g), dq_pair.at[i, :, cols(g, gw)], rq_send.at[i, g], rq_recv.at[i, g], sib
            )
            for i in range(2)
        ]

    def far_copy(g):
        return remote(part(dq, b_z, g), dq_far.at[:, cols(g, gw)], rz_send.at[g], rz_recv.at[g], zpart)

    def attention(g):
        gathered(g)

        @pl.loop(0, group)
        def _(i):
            h = g * group + i
            c = cols(h, HEAD_DIM)
            qh, gh = q_all[:, c], g_all[:, c]
            inv = inverse[pl.ds(h, 1), :]
            dl = jnp.concatenate([delta[g, b, pl.ds(i, 1), :] for b in range(4)], axis=1)
            q_acc = jnp.zeros((nq, HEAD_DIM), F32)
            for n in range(nkeys // part_keys):
                r = pl.ds(n * part_keys, part_keys)
                kh = k_all[r, c]
                p = probs[h, r, :].astype(F32) * inv
                s = (p * (dot_nt(v_all[r, c], gh) - dl)).astype(BF16)
                dv[r, c] = dot_nn(p.astype(BF16), gh).astype(BF16)
                dk[r, c] = (dot_nn(s, qh) * scale).astype(BF16)
                q_acc = q_acc + dot_tn(s, kh)
            dq[:, c] = (q_acc * scale).astype(BF16)

        for w in range(2):
            for c in x_first(w, g):
                c.start()
        for c in pair_copies(g):
            c.start()

    def second_step(g):
        for c in pair_copies(g):
            c.wait_recv()
        rows_z = pl.ds(pl.multiple_of(b_z * tok, tok), tok)
        dq[rows_z, cols(g, gw)] = (
            dq[rows_z, cols(g, gw)].astype(F32) + dq_pair[1 - zl, :, cols(g, gw)].astype(F32)
        ).astype(BF16)
        far_copy(g).start()

    def first_sent():
        def sent(dy, n):
            a2a(0, dy, n).wait_send()
            a2a(1, dy, n).wait_send()

        chunks(0, ny, sent)
        for c in q_sends:
            c.wait_send()
        q_forward().wait_send()
        for which in range(2):
            for k in range(1, nx):
                kv_copy(which, k).wait_send()
        for k in range(1, 4):
            sum_copy(k).wait_send()

    def back_sent(g):
        chunks(0, ny, lambda dy, n: back_copy(g, dy, n).wait_send())

    def group_sent(g):
        for c in g_sends(g):
            c.wait_send()
        g_forward(g).wait_send()
        for k in range(1, 4):
            delta_copy(g, k).wait_send()
        for c in pair_copies(g):
            c.wait_send()
        for w in range(2):
            for c in x_first(w, g) + x_second(w, g):
                c.wait_send()
        far_copy(g).wait_send()

    @pl.loop(0, ngroup + LAG)
    def _(step):
        @pl.when((step >= 1) & (step <= ngroup))
        def _():
            forward(step - 1)

        @pl.when(step < ngroup)
        def _():
            combine(step)

        @pl.when((step >= 1) & (step <= ngroup))
        def _():
            attention(step - 1)

        @pl.when((step >= 2) & (step < ngroup + 2))
        def _():
            second_step(step - 2)

        @pl.when(step == 1)
        def _():
            w_relay()

        @pl.when(step >= LAG)
        def _():
            x_relay(step - LAG)

        @pl.when(step == 2)
        def _():
            first_sent()

        @pl.when(step == ngroup)
        def _():
            w_over_z()

            @pl.loop(0, ngroup)
            def _(g):
                back_sent(g)

            for w in range(2):
                for c in w_first(w) + w_second(w):
                    c.wait_send()

    rows_x = pl.ds(pl.multiple_of(my_x * tok, tok), tok)

    @pl.loop(0, ngroup)
    def _(g):
        c = cols(g, gw)

        @pl.when(g > 0)
        def _():
            group_sent(g - 1)

        far_copy(g).wait_recv()
        dq[mine, c] = (
            dq[mine, c].astype(F32) + dq_pair[zl, :, c].astype(F32) + dq_far[:, c].astype(F32)
        ).astype(BF16)
        for w, (src, far, _) in enumerate(kv_parts):
            for d in x_first(w, g)[2:] + x_second(w, g):
                d.wait_recv()
            src[rows_x, c] = (
                src[rows_x, c].astype(F32) + far[0, :, c].astype(F32) + far[1, :, c].astype(F32)
            ).astype(BF16)

    outs = [
        pltpu.make_async_copy(blk(dq, b_me), qg_ref, out_sem.at[0]),
        pltpu.make_async_copy(blk(dk, my_x), kg_ref, out_sem.at[1]),
        pltpu.make_async_copy(blk(dv, my_x), vg_ref, out_sem.at[2]),
    ]
    for c in outs:
        c.start()
    for c in w_z:
        c.wait()
    out1[...] = (t1[core, zl].astype(F32) + t1_z[...].astype(F32)).astype(BF16)
    out2[...] = (t2[core, zl].astype(F32) + t2_z[...].astype(F32)).astype(BF16)
    outs += [
        pltpu.make_async_copy(out1, w1g_ref, out_sem.at[3]),
        pltpu.make_async_copy(out2, w2g_ref, out_sem.at[4]),
    ]
    for c in outs[3:]:
        c.start()

    for g in range(ngroup - 1, ngroup):
        group_sent(g)

    for c in outs:
        c.wait()


def hand_out(*refs):
    n = len(refs) // 2
    for i in range(n):
        refs[n + i][...] = refs[i][...]


def per_device(queries, key_states, value_states, attended, output_grad, expert_ids, gate_weights, w_in, w_out):
    tok, width = queries.shape[1:]
    ff = w_in.shape[2]
    heads = width // HEAD_DIM
    nexp, nctx = lax.axis_size("exp"), lax.axis_size("ctx")
    nx, ny = nctx // 4, nexp // 4
    cap = 3 * tok // nexp
    pairs = nexp * cap
    group = 3 if heads % 3 == 0 else 2
    ngroup, gw = heads // group, group * HEAD_DIM
    hp = -(-heads // 8) * 8
    wr1, wr2 = width // nctx, ff // nctx
    dma = pltpu.SemaphoreType.DMA
    v = pltpu.VMEM
    scratch = [
        v((tok, width), BF16), v((tok, width), BF16), v((width, ff), BF16), v((ff, width), BF16),
        v((nexp, tok), F32), v((nexp, tok), F32), v((pairs, tok), BF16), v((tok, pairs), BF16),
        v((pairs, tok), F32), v((pairs, width), F32),
        v((nexp, cap, width), BF16), v((nexp, cap, width), BF16), v((ngroup, nexp, cap, gw), BF16),
        v((nexp, cap, width), BF16), v((nexp, cap, width), BF16), v((ngroup, nexp, cap, gw), BF16),
        v((pairs, width), BF16), v((pairs, width), BF16), v((pairs // 2, ff), F32), v((pairs, ff), BF16), v((pairs, ff), BF16),
        v((pairs, gw), F32), v((pairs, gw), BF16),
        v((4 * tok, width), BF16), v((nx * tok, width), BF16), v((nx * tok, width), BF16), v((4 * tok, width), BF16),
        v((heads, nx * tok, 4 * tok), BF16),
        v((hp, 4 * tok), F32), v((4, hp, 4 * tok), F32), v((hp, 4 * tok), F32), v((ngroup, 4, 8, tok), F32),
        v((4 * tok, width), BF16), v((nx * tok, width), BF16), v((nx * tok, width), BF16),
        v((2, tok, width), BF16), v((tok, width), BF16),
        v((2, tok, width), BF16), v((2, tok, width), BF16),
        v((2, tok // 2, width), BF16), v((2, tok // 2, width), BF16),
        v((2, 2 * nx, wr1, ff), BF16), v((2, 2 * nx, wr2, width), BF16),
        v((2 * nx, wr1, ff), BF16), v((2 * nx, wr2, width), BF16),
        v((2, 2, wr1, ff), BF16), v((2, 2, wr2, width), BF16), v((2, wr1, ff), BF16), v((2, wr2, width), BF16),
        v((wr1, ff), BF16), v((wr2, width), BF16), v((wr1, ff), BF16), v((wr2, width), BF16),
        dma((7,)), dma((5,)), dma((2, nexp)), dma((2, nexp)), dma((ngroup, nexp)), dma((ngroup, nexp)), dma((2, nx)), dma((2, nx)),
        dma((3,)), dma((3,)), dma((3, ngroup)), dma((3, ngroup)), dma((4,)), dma((4,)), dma((ngroup, 4)), dma((ngroup, 4)),
        dma((2, 6, ngroup)), dma((2, 6, ngroup)), dma((2, ngroup)), dma((2, ngroup)),
        dma((ngroup,)), dma((ngroup,)), dma((4,)), dma((4,)), dma((2, 6)), dma((2, 6)),
    ]
    block = jax.ShapeDtypeStruct((tok, width), BF16)
    shapes = [block, block, block, jax.ShapeDtypeStruct((wr1, ff), BF16), jax.ShapeDtypeStruct((wr2, width), BF16)]
    hbm = pl.BlockSpec(memory_space=pl.ANY)
    small = pl.BlockSpec(memory_space=pltpu.VMEM)
    results = pl.pallas_call(
        functools.partial(kernel, nx, ny, nexp, group),
        out_shape=shapes,
        in_specs=[small] * 2 + [hbm] * 7,
        out_specs=[hbm] * 5,
        scratch_shapes=scratch,
        compiler_params=pltpu.CompilerParams(
            collective_id=0, has_side_effects=True, vmem_limit_bytes=60 * 1024 * 1024
        ),
        name="block_backward",
    )(
        expert_ids[0].T, gate_weights[0].T, queries[0], key_states[0], value_states[0], attended[0], output_grad[0],
        w_in[0], w_out[0],
    )
    results = pl.pallas_call(
        hand_out, out_shape=shapes, in_specs=[small] * 5, out_specs=[small] * 5, name="hand_out"
    )(*results)
    return tuple(r[None] for r in results)


def solution(mesh):
    stream = P("exp", "ctx", None)
    return jax.shard_map(
        per_device,
        mesh=mesh,
        in_specs=(stream,) * 7 + (P("exp", None, None),) * 2,
        out_specs=(stream,) * 5,
        check_vma=False,
    )
```
